32 devices in a mesh: spin: 2 (over x), orb: 16 (over z, y, core).
Axes of the slice: x: 2, y: 2, z: 4, core: 2. Of those that a mesh axis runs over, the one named last changes fastest.
Arguments:
- integrals: bfloat16 [2, 16, 256, 512], P('spin', None, None, 'orb'), may hold values from -0.875 to 0.875
- metric_factor: bfloat16 [512, 512], replicated, may hold values from -0.25 to 0.25
- occ_energy: float32 [2, 16], replicated, may hold values from -2.5 to -0.3
- virt_energy: float32 [2, 256], replicated, may hold values from 0.3 to 3
Outputs:
- gamma_out: float32 [2, 16, 256, 512], P('spin', 'orb')
- density: float32 [2, 256, 256], P('spin', 'orb')
The draws below stay inside these ranges and needn't reach their ends.
All inputs are finite; a program needn't handle non-finite values.
Results may differ from the reference program's by a relative error of at most 0.0019.
Values may be sent and summed in bfloat16 or wider, within the bound.
No kernel may reach another device: no remote copies, remote signals or barrier semaphores. Data moves between devices by JAX's collectives and lax.ppermute only.
A program may use at most 192 MiB of HBM per device.

```python
import jax
import jax.numpy as jnp
from jax import lax

NV = 256
NAUX = 512
OCC = 16


def block_levels(own_key, shape, pieces, least, largest):
    def one(dim, parts):
        steps = jax.random.uniform(jax.random.fold_in(jax.random.fold_in(own_key, 6), dim), (parts,), jnp.float32, least / len(pieces), largest / len(pieces))
        return jnp.repeat(jnp.exp(steps), shape[dim] // parts).reshape((-1,) + (1,) * (len(shape) - dim - 1))

    factor_of = one(*pieces[0])
    for cut in pieces[1:]:
        factor_of = factor_of * one(*cut)
    return factor_of


def bell_draw(rng, extent, scale, reach, shards=(), kind=jnp.bfloat16):
    factor_of = block_levels(rng, extent, shards, -0.22, 0.18) if shards else 1.0
    array = jax.random.normal(rng, extent, jnp.float32) * scale * factor_of
    return jnp.minimum(jnp.maximum(array, -reach), reach).astype(kind)


def setup_inputs(seed: int = 0) -> dict:
    key_of = jax.random.split(jax.random.key(seed), 5)
    integrals = bell_draw(key_of[0], (2, OCC, NV, NAUX), 0.06, 0.875, ((0, 2), (3, 16)))
    metric_factor = bell_draw(key_of[1], (NAUX, NAUX), NAUX ** -0.5, 0.25)
    occ_energy = jnp.clip(jax.random.uniform(key_of[2], (2, OCC), jnp.float32, -2.5, -0.3), -2.5, -0.3)
    virt_energy = jnp.clip(jax.random.uniform(key_of[3], (2, NV), jnp.float32, 0.3, 3.0), 0.3, 3.0)
    return {"integrals": integrals, "metric_factor": metric_factor, "occ_energy": occ_energy, "virt_energy": virt_energy}


def pair_terms(left_block, right_blocks, e_left, e_right, v_left, v_right, antisym, weight_value):
    coupling = jnp.einsum('aq,jbq->jab', left_block, right_blocks)
    if antisym:
        coupling = coupling - jnp.swapaxes(coupling, 1, 2)
    denominator = e_left + e_right[:, None, None] - v_left[None, :, None] - v_right[None, None, :]
    amplitude = (coupling / denominator).astype(jnp.bfloat16)
    amplitude = lax.optimization_barrier(amplitude).astype(jnp.float32)
    gamma_terms = jnp.einsum('jab,jbq->aq', amplitude, right_blocks)
    density_terms = jnp.einsum('jac,jbc->ab', weight_value * amplitude, amplitude)
    return gamma_terms, density_terms


def reference(integrals, metric_factor, occ_energy, virt_energy):
    fitted_list = []
    for spin_index in range(2):
        flat = integrals[spin_index].reshape(OCC * NV, NAUX)
        product = jnp.dot(flat, metric_factor, preferred_element_type=jnp.float32)
        fitted_list.append(product.astype(jnp.bfloat16).reshape(OCC, NV, NAUX))
    gamma_list = []
    density_list = []
    for spin_index in range(2):
        other_spin = 1 - spin_index
        same_blocks = fitted_list[spin_index].astype(jnp.float32)
        other_blocks = fitted_list[other_spin].astype(jnp.float32)

        def one_row(totals, row_index):
            left_block = lax.dynamic_index_in_dim(same_blocks, row_index, 0, keepdims=False)
            e_left = lax.dynamic_index_in_dim(occ_energy[spin_index], row_index, 0, keepdims=False)
            gamma_same, density_same = pair_terms(left_block, same_blocks, e_left, occ_energy[spin_index], virt_energy[spin_index], virt_energy[spin_index], True, 0.5)
            gamma_other, density_other = pair_terms(left_block, other_blocks, e_left, occ_energy[other_spin], virt_energy[spin_index], virt_energy[other_spin], False, 1.0)
            return totals + density_same + density_other, gamma_same + gamma_other

        density_sum, gamma_rows = lax.scan(one_row, jnp.zeros((NV, NV), jnp.float32), jnp.arange(OCC, dtype=jnp.int32))
        gamma_list.append(gamma_rows)
        density_list.append(density_sum / OCC)
    return jnp.stack(gamma_list), jnp.stack(density_list)
```

```python
import functools

import jax
import jax.numpy as jnp
import numpy as np
from jax import lax
from jax.experimental import pallas as pl
from jax.experimental.pallas import tpu as pltpu
from jax.sharding import PartitionSpec as P

VMEM_LIMIT = 48 * 1024 * 1024
NN = (((1,), (0,)), ((), ()))
NT = (((1,), (1,)), ((), ()))
TN = (((0,), (0,)), ((), ()))


def dot(left, right, dims):
    return lax.dot_general(left, right, dims, preferred_element_type=jnp.float32)


def chip_ring(orb_count):
    chips = orb_count // 2
    order = list(range(0, chips, 2)) + list(range(chips - 1 - chips % 2, 0, -2))
    following = {order[r]: order[(r + 1) % chips] for r in range(chips)}
    return order, following


def ring_moves(orb_count):
    _, following = chip_ring(orb_count)
    forward = [(2 * p, 2 * q) for p, q in following.items()]
    backward = [(2 * q + 1, 2 * p + 1) for p, q in following.items()]
    return forward + backward


def slice_sources(orb_count):
    order, _ = chip_ring(orb_count)
    chips = len(order)
    place = {chip: r for r, chip in enumerate(order)}
    table = []
    for device in range(orb_count):
        chip, core = device // 2, device % 2
        sources = [device, device ^ 1]
        for step in range(1, chips // 2 + 1):
            ahead = order[(place[chip] + (step if core else -step)) % chips]
            behind = order[(place[chip] - (step if core else -step)) % chips]
            if 2 * step == chips:
                sources += [2 * ahead + core, 2 * behind + 1 - core]
            else:
                sources += [2 * ahead + core, 2 * ahead + 1 - core]
                sources += [2 * behind + 1 - core, 2 * behind + core]
        table.append(sources)
    return np.asarray(table, np.int32)


def gather_slices(own, orb_count):
    moves = ring_moves(orb_count)
    swap = [(d, d ^ 1) for d in range(orb_count)]
    chips = orb_count // 2
    lanes = [own, lax.ppermute(own, "orb", swap)]
    gathered = list(lanes)
    for step in range(1, chips // 2 + 1):
        if 2 * step == chips:
            lanes = lanes[:1]
        lanes = [lax.ppermute(lane, "orb", moves) for lane in lanes]
        swapped = lax.ppermute(jnp.stack(lanes), "orb", swap)
        gathered += lanes + [swapped[n] for n in range(len(lanes))]
    return gathered


def fit_kernel(factor_ref, *refs):
    slices, out_ref = refs[:-1], refs[-1]
    for g in range(out_ref.shape[0]):
        raw = jnp.concatenate([piece[g] for piece in slices], axis=0)
        out_ref[g] = dot(factor_ref[...], raw, NN).astype(out_ref.dtype)


def fit(factor, slices, group):
    count, _, virt = slices[0].shape
    naux = factor.shape[0]
    return pl.pallas_call(
        fit_kernel,
        grid=(count // group,),
        in_specs=[pl.BlockSpec(factor.shape, lambda j: (0, 0))]
        + [pl.BlockSpec((group,) + s.shape[1:], lambda j: (j, 0, 0)) for s in slices],
        out_specs=pl.BlockSpec((group, naux, virt), lambda j: (j, 0, 0)),
        out_shape=jax.ShapeDtypeStruct((count, naux, virt), jnp.bfloat16),
        compiler_params=pltpu.CompilerParams(vmem_limit_bytes=VMEM_LIMIT),
        name="fit",
    )(factor, *slices)


def same_kernel(own_ref, pair_ref, own_block, blocks, v_col, v_row, gamma_ref, dens_ref, left):
    step = pl.program_id(0)

    @pl.when(step == 0)
    def _():
        left[...] = own_block[0].T
        gamma_ref[...] = jnp.zeros_like(gamma_ref)
        dens_ref[...] = jnp.zeros_like(dens_ref)

    group = blocks.shape[0]
    for g in range(group):
        right = blocks[g]
        coupling = dot(left[...], right, NN)
        coupling = coupling - coupling.T
        denominator = (pair_ref[step * group + g] - v_col[...]) - v_row[...]
        amplitude = (coupling / denominator).astype(jnp.bfloat16)
        gamma_ref[...] += dot(amplitude, right, NT)
        dens_ref[...] += 0.5 * dot(amplitude, amplitude, NT)


def same_spin(fitted, own_index, pair_energy, virt, group):
    count, naux, nv = fitted.shape
    whole = lambda shape: pl.BlockSpec(shape, lambda j, *_: (0,) * len(shape))
    return pl.pallas_call(
        same_kernel,
        grid_spec=pltpu.PrefetchScalarGridSpec(
            num_scalar_prefetch=2,
            grid=(count // group,),
            in_specs=[
                pl.BlockSpec((1, naux, nv), lambda j, own, pair: (own[0], 0, 0)),
                pl.BlockSpec((group, naux, nv), lambda j, own, pair: (j, 0, 0)),
                whole((nv, 1)),
                whole((1, nv)),
            ],
            out_specs=[whole((nv, naux)), whole((nv, nv))],
            scratch_shapes=[pltpu.VMEM((nv, naux), jnp.bfloat16)],
        ),
        out_shape=[
            jax.ShapeDtypeStruct((nv, naux), jnp.float32),
            jax.ShapeDtypeStruct((nv, nv), jnp.float32),
        ],
        compiler_params=pltpu.CompilerParams(vmem_limit_bytes=VMEM_LIMIT),
        name="same_spin",
    )(own_index, pair_energy, fitted, fitted, virt[:, None], virt[None, :])


def opposite_kernel(pair_ref, factor, raw, blocks, v_col, v_row, dens_in, gamma_ref, dens_ref, left):
    step = pl.program_id(0)

    @pl.when(step == 0)
    def _():
        left[...] = dot(factor[...], raw[...], NN).astype(left.dtype).T
        gamma_ref[...] = jnp.zeros_like(gamma_ref)
        dens_ref[...] = dens_in[...]

    group = blocks.shape[0]
    for g in range(group):
        right = blocks[g]
        coupling = dot(left[...], right, NN)
        denominator = (pair_ref[step * group + g] - v_col[...]) - v_row[...]
        amplitude = (coupling / denominator).astype(jnp.bfloat16)
        gamma_ref[...] += dot(amplitude, right, NT)
        dens_ref[...] += dot(amplitude, amplitude, TN)


def opposite_spin(fitted, factor, raw, pair_energy, virt_left, virt_right, dens, group):
    count, naux, nv = fitted.shape
    whole = lambda shape: pl.BlockSpec(shape, lambda j, *_: (0,) * len(shape))
    return pl.pallas_call(
        opposite_kernel,
        grid_spec=pltpu.PrefetchScalarGridSpec(
            num_scalar_prefetch=1,
            grid=(count // group,),
            in_specs=[
                whole(factor.shape),
                whole(raw.shape),
                pl.BlockSpec((group, naux, nv), lambda j, pair: (j, 0, 0)),
                whole((nv, 1)),
                whole((1, nv)),
                whole((nv, nv)),
            ],
            out_specs=[whole((nv, naux)), whole((nv, nv))],
            scratch_shapes=[pltpu.VMEM((nv, naux), jnp.bfloat16)],
        ),
        out_shape=[
            jax.ShapeDtypeStruct((nv, naux), jnp.float32),
            jax.ShapeDtypeStruct((nv, nv), jnp.float32),
        ],
        compiler_params=pltpu.CompilerParams(vmem_limit_bytes=VMEM_LIMIT),
        name="opposite_spin",
    )(pair_energy, factor, raw, fitted, virt_left[:, None], virt_right[None, :], dens)


def reduce_rows(total, orb_count):
    index = lax.axis_index("orb")
    bits = orb_count.bit_length() - 1
    rows = total.reshape((2,) * bits + (total.shape[0] // orb_count, total.shape[1]))
    for bit in range(bits):
        axis = bits - 1 - bit
        mine = (index >> bit) & 1
        moves = [(d, d ^ (1 << bit)) for d in range(orb_count)]
        kept = lax.dynamic_index_in_dim(rows, mine, axis, keepdims=False)
        sent = lax.dynamic_index_in_dim(rows, 1 - mine, axis, keepdims=False)
        rows = kept + lax.ppermute(sent, "orb", moves)
    return rows


def local(integrals, metric_factor, occ_energy, virt_energy, orb_count):
    spin_index = lax.axis_index("spin")
    orbit_index = lax.axis_index("orb")
    other_spin = 1 - spin_index
    pick = lambda array, n: lax.dynamic_index_in_dim(array, n, 0, keepdims=False)
    occ_same, occ_other = pick(occ_energy, spin_index), pick(occ_energy, other_spin)
    virt_same, virt_other = pick(virt_energy, spin_index), pick(virt_energy, other_spin)
    across = [(0, 1), (1, 0)]

    own = jnp.swapaxes(integrals[0], 1, 2)
    occupied, width, nv = own.shape
    naux = metric_factor.shape[0]
    sources = pick(jnp.asarray(slice_sources(orb_count)), orbit_index)
    factor = jnp.take(metric_factor.reshape(orb_count, width, naux), sources, axis=0)
    factor = factor.reshape(naux, naux).T

    slices = gather_slices(own, orb_count)
    own_row = [pick(s, orbit_index) for s in slices]
    early = len(slices) - 6 if len(slices) > 8 else len(slices) // 2
    raw_row = jnp.concatenate(
        [
            lax.ppermute(jnp.concatenate(own_row[:early]), "spin", across),
            lax.ppermute(jnp.concatenate(own_row[early:]), "spin", across),
        ]
    )
    if width % 16:
        slices = [jnp.concatenate(slices, axis=1)]
    fitted = fit(factor, slices, 2)

    own_energy, other_energy = pick(occ_same, orbit_index), pick(occ_other, orbit_index)
    gamma_same, dens = same_spin(fitted, orbit_index[None], own_energy + occ_same, virt_same, 2)
    gamma_other, dens = opposite_spin(
        fitted, factor, raw_row, other_energy + occ_same, virt_other, virt_same, dens, 2
    )
    returned = lax.ppermute(gamma_other, "spin", across)
    gamma = gamma_same + returned
    density = reduce_rows(dens, orb_count) / occupied
    return gamma[None, None], density[None]


def solution(mesh):
    return jax.shard_map(
        functools.partial(local, orb_count=mesh.shape["orb"]),
        mesh=mesh,
        in_specs=(P("spin", None, None, "orb"), P(), P(), P()),
        out_specs=(P("spin", "orb", None, None), P("spin", "orb", None)),
        check_vma=False,
    )
```

```python
import functools

import jax
import jax.numpy as jnp
import numpy as np
from jax import lax
from jax.experimental import pallas as pl
from jax.experimental.pallas import tpu as pltpu
from jax.sharding import PartitionSpec as P

VMEM_LIMIT = 20 * 1024 * 1024
GROUP = 4
NN = (((1,), (0,)), ((), ()))
NT = (((1,), (1,)), ((), ()))
TN = (((0,), (0,)), ((), ()))


def dot(left, right, dims):
    return lax.dot_general(left, right, dims, preferred_element_type=jnp.float32)


def chip_ring(orb_count):
    chips = orb_count // 2
    order = list(range(0, chips, 2)) + list(range(chips - 1 - chips % 2, 0, -2))
    following = {order[r]: order[(r + 1) % chips] for r in range(chips)}
    return order, following


def ring_moves(orb_count):
    _, following = chip_ring(orb_count)
    forward = [(2 * p, 2 * q) for p, q in following.items()]
    backward = [(2 * q + 1, 2 * p + 1) for p, q in following.items()]
    return forward + backward


def slice_sources(orb_count):
    order, _ = chip_ring(orb_count)
    chips = len(order)
    place = {chip: r for r, chip in enumerate(order)}
    table = []
    for device in range(orb_count):
        chip, core = device // 2, device % 2
        sources = [device, device ^ 1]
        for step in range(1, chips // 2 + 1):
            ahead = order[(place[chip] + (step if core else -step)) % chips]
            behind = order[(place[chip] - (step if core else -step)) % chips]
            if 2 * step == chips:
                sources += [2 * ahead + core, 2 * behind + 1 - core]
            else:
                sources += [2 * ahead + core, 2 * ahead + 1 - core]
                sources += [2 * behind + 1 - core, 2 * behind + core]
        table.append(sources)
    return np.asarray(table, np.int32)


def gather_slices(own, orb_count):
    moves = ring_moves(orb_count)
    swap = [(d, d ^ 1) for d in range(orb_count)]
    chips = orb_count // 2
    lanes = [own, lax.ppermute(own, "orb", swap)]
    gathered = list(lanes)
    for step in range(1, chips // 2 + 1):
        if 2 * step == chips:
            lanes = lanes[:1]
        lanes = [lax.ppermute(lane, "orb", moves) for lane in lanes]
        swapped = lax.ppermute(jnp.stack(lanes), "orb", swap)
        gathered += lanes + [swapped]
    return gathered


def pieces(refs, orbital):
    for ref in refs:
        if len(ref.shape) == 3:
            yield ref[orbital]
        else:
            for lane in range(ref.shape[0]):
                yield ref[lane, orbital]


def order_factor(factor_ref, rows, orb_count):
    own = lax.axis_index("orb")
    chips, width = orb_count // 2, factor_ref.shape[0] // orb_count
    chip, core = own // 2, own % 2
    place = jnp.where(chip % 2 == 0, chip // 2, chips - (chip + 1) // 2)

    def chip_at(distance):
        there = (place + chips + jnp.where(core == 0, -distance, distance)) % chips
        return jnp.where(2 * there < chips, 2 * there, 2 * (chips - there) - 1)

    sources = [own, own ^ 1]
    for step in range(1, chips // 2 + 1):
        ahead, behind = 2 * chip_at(step), 2 * chip_at(-step)
        if 2 * step == chips:
            sources += [ahead + core, behind + 1 - core]
        else:
            sources += [ahead + core, ahead + 1 - core, behind + 1 - core, behind + core]
    for n, source in enumerate(sources):
        rows[n * width : (n + 1) * width] = factor_ref[pl.ds(pl.multiple_of(source * width, width), width)]
    return rows[...].T


def row_kernel(*refs):
    *slices, out_ref = refs
    out_ref[...] = jnp.concatenate(list(pieces(slices, lax.axis_index("orb"))), axis=0)


def early_row_kernel(own_hbm, *refs):
    *slices, out_ref, own_ref, arrived = refs
    fetch = pltpu.make_async_copy(own_hbm, own_ref, arrived)
    fetch.start()
    fetch.wait()
    out_ref[...] = jnp.concatenate(list(pieces([own_ref] + slices, lax.axis_index("orb"))), axis=0)


def stack_kernel(lanes, *refs):
    for n in range(lanes):
        refs[-1][n] = refs[n][...]


def energy_sums(virt_ref, left_spin, right_spin):
    nv = virt_ref.shape[1]
    left = jnp.broadcast_to(virt_ref[pl.ds(left_spin, 1)], (nv, nv)).T
    return left + virt_ref[pl.ds(right_spin, 1)]


def pair_energies(occ_ref, left_spin, right_spin, own):
    left = occ_ref[pl.ds(left_spin, 1)]
    chosen = lax.broadcasted_iota(jnp.int32, left.shape, 1) == own
    return jnp.sum(jnp.where(chosen, left, 0.0), axis=1, keepdims=True) + occ_ref[pl.ds(right_spin, 1)]


def amplitudes(coupling, occupied_pair, virtual_pair):
    return (coupling / (occupied_pair - virtual_pair)).astype(jnp.bfloat16)


def fit_same_kernel(orb_count, occ_ref, virt_ref, given_ref, *refs):
    slices, (factor_ref, fitted_ref, gamma_ref, dens_ref) = refs[:-8], refs[-8:-4]
    rows, left, sums, amp_ref = refs[-4:]
    factor_ref[...] = order_factor(given_ref, rows, orb_count)
    spin, own = lax.axis_index("spin"), lax.axis_index("orb")
    count, nv = occ_ref.shape[1], virt_ref.shape[1]
    sums[...] = energy_sums(virt_ref, spin, spin)
    energies = pair_energies(occ_ref, spin, spin, own)
    raw = jnp.concatenate(list(pieces(slices, own)), axis=0)
    left[...] = dot(factor_ref[...], raw, NN).T.astype(left.dtype)
    total = None
    for start in range(0, count, GROUP):
        members = range(start, start + GROUP)
        raw = [jnp.concatenate(list(pieces(slices, j)), axis=0) for j in members]
        fitted = dot(factor_ref[...], jnp.concatenate(raw, axis=1), NN).astype(fitted_ref.dtype)
        columns = slice(start * nv, (start + GROUP) * nv)
        fitted_ref[:, columns] = fitted
        couplings = dot(left[...], fitted, NN)
        amps = []
        for n, j in enumerate(members):
            coupling = couplings[:, n * nv : (n + 1) * nv]
            amps.append(amplitudes(coupling - coupling.T, energies[:, j : j + 1], sums[...]))
        amps = jnp.concatenate(amps, axis=1)
        amp_ref[:, columns] = amps
        term = dot(amps, amps, NT)
        total = term if total is None else total + term
    dens_ref[...] = 0.5 * total
    gamma_ref[...] = dot(amp_ref[...], fitted_ref[...], NT)


def opposite_all_kernel(
    occ_ref, virt_ref, factor_ref, early_ref, late_ref, fitted_ref, dens_in,
    gamma_ref, kept_ref, sent_ref, left, sums, dens, amp_ref,
):
    spin, own = lax.axis_index("spin"), lax.axis_index("orb")
    count, nv = occ_ref.shape[1], virt_ref.shape[1]
    sums[...] = energy_sums(virt_ref, 1 - spin, spin)
    energies = pair_energies(occ_ref, 1 - spin, spin, own)
    raw = jnp.concatenate([early_ref[...], late_ref[...]], axis=0)
    left[...] = dot(factor_ref[...], raw, NN).T.astype(left.dtype)
    total = dens_in[...]
    for start in range(0, count, GROUP):
        columns = slice(start * nv, (start + GROUP) * nv)
        couplings = dot(left[...], fitted_ref[:, columns], NN)
        amps = []
        for n in range(GROUP):
            energy = energies[:, start + n : start + n + 1]
            amps.append(amplitudes(couplings[:, n * nv : (n + 1) * nv], energy, sums[...]))
        amp_ref[:, columns] = jnp.concatenate(amps, axis=1)
        stacked = jnp.concatenate(amps, axis=0)
        total = total + dot(stacked, stacked, TN)
    dens[...] = total / count
    core = own % 2
    chips, rows, _ = kept_ref.shape
    for chip in range(chips):
        for ref, lane in ((kept_ref, core), (sent_ref, 1 - core)):
            first = pl.multiple_of((2 * chip + lane) * rows, rows)
            ref[chip] = dens[pl.ds(first, rows)]
    gamma_ref[...] = dot(amp_ref[...], fitted_ref[...], NT).astype(gamma_ref.dtype)


def join_kernel(gamma_in, returned, kept_in, arrived, gamma_ref, kept_ref, sent_ref, total):
    gamma_ref[...] = gamma_in[...] + returned[...].astype(jnp.float32)
    total[...] = kept_in[...] + arrived[...]
    far = lax.axis_index("orb") // (lax.axis_size("orb") // 2)
    kept_ref[...] = total[far]
    sent_ref[...] = total[1 - far]


def vmem_call(kernel, name, operands, outs, scratch=(), flops=0, in_hbm=0, pin=True):
    vmem, hbm = pl.BlockSpec(memory_space=pltpu.VMEM), pl.BlockSpec(memory_space=pltpu.HBM)
    moved = sum(a.size * a.dtype.itemsize for a in operands)
    if pin:
        places = [pltpu.HBM] * in_hbm + [pltpu.VMEM] * (len(operands) - in_hbm)
        operands = [pltpu.with_memory_space_constraint(*pair) for pair in zip(operands, places)]
    return pl.pallas_call(
        kernel,
        in_specs=[hbm] * in_hbm + [vmem] * (len(operands) - in_hbm),
        out_specs=[vmem] * len(outs),
        out_shape=[pltpu.VMEM(*out) if pin else jax.ShapeDtypeStruct(*out) for out in outs],
        scratch_shapes=[pltpu.VMEM(*s) if isinstance(s, tuple) else s for s in scratch],
        compiler_params=pltpu.CompilerParams(vmem_limit_bytes=VMEM_LIMIT),
        cost_estimate=pl.CostEstimate(flops=flops, bytes_accessed=moved, transcendentals=0),
        name=name,
    )(*operands)


def local_in_vmem(integrals, metric_factor, occ_energy, virt_energy, orb_count):
    across = [(0, 1), (1, 0)]
    swap = [(d, d ^ 1) for d in range(orb_count)]
    moves = ring_moves(orb_count)
    own = jnp.swapaxes(integrals[0], 1, 2)
    count, width, nv = own.shape
    naux = metric_factor.shape[0]
    half, full, arrival = jnp.bfloat16, jnp.float32, pltpu.SemaphoreType.DMA
    depth = lambda part: width * sum(1 if s.ndim == 3 else s.shape[0] for s in part)

    steps = orb_count // 4
    lanes = [own, lax.ppermute(own, "orb", swap)]
    slices, sent, early_row = list(lanes), 0, None
    for step in range(1, steps + 1):
        lanes = [lax.ppermute(lane, "orb", moves) for lane in (lanes if step < steps else lanes[:1])]
        slices += lanes
        if step == steps-3:
            sent = len(slices)
            row, own = vmem_call(
                early_row_kernel, "early_row", slices, [((depth(slices), nv), half), (own.shape, half)],
                [arrival], in_hbm=1,
            )
            early_row = lax.ppermute(row, "spin", across)
            slices[0] = own
        order = [early_row] if step == steps-1 else []
        (stacked,) = vmem_call(
            functools.partial(stack_kernel, len(lanes)), "stack", lanes + order,
            [((len(lanes),) + own.shape, half)],
        )
        slices.append(lax.ppermute(stacked, "orb", swap))
    (row,) = vmem_call(row_kernel, "late_row", slices[sent:], [((depth(slices[sent:]), nv), half)])
    late_row = lax.ppermute(row, "spin", across)
    pair = 2 * count * nv * nv
    factor, fitted, gamma_same, dens_same = vmem_call(
        functools.partial(fit_same_kernel, orb_count), "fit_same",
        [occ_energy, virt_energy, metric_factor] + slices,
        [((naux, naux), half), ((naux, count * nv), half), ((nv, naux), full), ((nv, nv), full)],
        [((naux, naux), half), ((nv, naux), half), ((nv, nv), full), ((nv, count * nv), half)],
    )
    rows = nv // orb_count
    gamma_other, kept, sent = vmem_call(
        opposite_all_kernel, "opposite",
        [occ_energy, virt_energy, factor, early_row, late_row, fitted, dens_same],
        [((nv, naux), half)] + [((orb_count // 2, rows, nv), full)] * 2,
        [((nv, naux), half), ((nv, nv), full), ((nv, nv), full), ((nv, count * nv), half)],
        flops=pair * (2 * naux + nv),
    )
    returned = lax.ppermute(gamma_other, "spin", across)
    kept, arrived = reduce_rows(kept + lax.ppermute(sent, "orb", swap), orb_count, 2)
    gamma, kept, sent = vmem_call(
        join_kernel, "join", [gamma_same, returned, kept, arrived],
        [((nv, naux), full)] + [((rows, nv), full)] * 2, [((2, rows, nv), full)], pin=False,
    )
    far = [(d, d ^ (orb_count // 2)) for d in range(orb_count)]
    density = kept + lax.ppermute(sent, "orb", far)
    return gamma[None, None], density[None]


def fit_kernel(factor_ref, *refs):
    slices, out_ref = refs[:-1], refs[-1]
    for g in range(out_ref.shape[0]):
        raw = jnp.concatenate([piece[g] for piece in slices], axis=0)
        out_ref[g] = dot(factor_ref[...], raw, NN).astype(out_ref.dtype)


def fit(factor, slices, group):
    count, _, virt = slices[0].shape
    naux = factor.shape[0]
    return pl.pallas_call(
        fit_kernel,
        grid=(count // group,),
        in_specs=[pl.BlockSpec(factor.shape, lambda j: (0, 0))]
        + [pl.BlockSpec((group,) + s.shape[1:], lambda j: (j, 0, 0)) for s in slices],
        out_specs=pl.BlockSpec((group, naux, virt), lambda j: (j, 0, 0)),
        out_shape=jax.ShapeDtypeStruct((count, naux, virt), jnp.bfloat16),
        compiler_params=pltpu.CompilerParams(vmem_limit_bytes=VMEM_LIMIT),
        name="fit",
    )(factor, *slices)


def same_kernel(own_ref, pair_ref, own_block, blocks, v_col, v_row, gamma_ref, dens_ref, left):
    step = pl.program_id(0)

    @pl.when(step == 0)
    def _():
        left[...] = own_block[0].T
        gamma_ref[...] = jnp.zeros_like(gamma_ref)
        dens_ref[...] = jnp.zeros_like(dens_ref)

    group = blocks.shape[0]
    for g in range(group):
        right = blocks[g]
        coupling = dot(left[...], right, NN)
        coupling = coupling - coupling.T
        denominator = (pair_ref[step * group + g] - v_col[...]) - v_row[...]
        amplitude = (coupling / denominator).astype(jnp.bfloat16)
        gamma_ref[...] += dot(amplitude, right, NT)
        dens_ref[...] += 0.5 * dot(amplitude, amplitude, NT)


def same_spin(fitted, own_index, pair_energy, virt, group):
    count, naux, nv = fitted.shape
    whole = lambda shape: pl.BlockSpec(shape, lambda j, *_: (0,) * len(shape))
    return pl.pallas_call(
        same_kernel,
        grid_spec=pltpu.PrefetchScalarGridSpec(
            num_scalar_prefetch=2,
            grid=(count // group,),
            in_specs=[
                pl.BlockSpec((1, naux, nv), lambda j, own, pair: (own[0], 0, 0)),
                pl.BlockSpec((group, naux, nv), lambda j, own, pair: (j, 0, 0)),
                whole((nv, 1)),
                whole((1, nv)),
            ],
            out_specs=[whole((nv, naux)), whole((nv, nv))],
            scratch_shapes=[pltpu.VMEM((nv, naux), jnp.bfloat16)],
        ),
        out_shape=[
            jax.ShapeDtypeStruct((nv, naux), jnp.float32),
            jax.ShapeDtypeStruct((nv, nv), jnp.float32),
        ],
        compiler_params=pltpu.CompilerParams(vmem_limit_bytes=VMEM_LIMIT),
        name="same_spin",
    )(own_index, pair_energy, fitted, fitted, virt[:, None], virt[None, :])


def opposite_kernel(pair_ref, factor, raw, blocks, v_col, v_row, dens_in, gamma_ref, dens_ref, left):
    step = pl.program_id(0)

    @pl.when(step == 0)
    def _():
        left[...] = dot(factor[...], raw[...], NN).astype(left.dtype).T
        gamma_ref[...] = jnp.zeros_like(gamma_ref)
        dens_ref[...] = dens_in[...]

    group = blocks.shape[0]
    for g in range(group):
        right = blocks[g]
        coupling = dot(left[...], right, NN)
        denominator = (pair_ref[step * group + g] - v_col[...]) - v_row[...]
        amplitude = (coupling / denominator).astype(jnp.bfloat16)
        gamma_ref[...] += dot(amplitude, right, NT)
        dens_ref[...] += dot(amplitude, amplitude, TN)


def opposite_spin(fitted, factor, raw, pair_energy, virt_left, virt_right, dens, group):
    count, naux, nv = fitted.shape
    whole = lambda shape: pl.BlockSpec(shape, lambda j, *_: (0,) * len(shape))
    return pl.pallas_call(
        opposite_kernel,
        grid_spec=pltpu.PrefetchScalarGridSpec(
            num_scalar_prefetch=1,
            grid=(count // group,),
            in_specs=[
                whole(factor.shape),
                whole(raw.shape),
                pl.BlockSpec((group, naux, nv), lambda j, pair: (j, 0, 0)),
                whole((nv, 1)),
                whole((1, nv)),
                whole((nv, nv)),
            ],
            out_specs=[whole((nv, naux)), whole((nv, nv))],
            scratch_shapes=[pltpu.VMEM((nv, naux), jnp.bfloat16)],
        ),
        out_shape=[
            jax.ShapeDtypeStruct((nv, naux), jnp.float32),
            jax.ShapeDtypeStruct((nv, nv), jnp.float32),
        ],
        compiler_params=pltpu.CompilerParams(vmem_limit_bytes=VMEM_LIMIT),
        name="opposite_spin",
    )(pair_energy, factor, raw, fitted, virt_left[:, None], virt_right[None, :], dens)


def reduce_rows(total, orb_count, keep):
    index = lax.axis_index("orb")
    bits = orb_count.bit_length() - 1
    rows = total.reshape((2,) * (bits - 1) + total.shape[1:])
    for bit in range(1, bits + 1 - keep.bit_length()):
        axis = bits - 1 - bit
        mine = (index >> bit) & 1
        moves = [(d, d ^ (1 << bit)) for d in range(orb_count)]
        kept = lax.dynamic_index_in_dim(rows, mine, axis, keepdims=False)
        sent = lax.dynamic_index_in_dim(rows, 1 - mine, axis, keepdims=False)
        arrived = lax.ppermute(sent, "orb", moves)
        rows = kept + arrived
    return kept, arrived


def local_streamed(integrals, metric_factor, occ_energy, virt_energy, orb_count):
    spin_index = lax.axis_index("spin")
    orbit_index = lax.axis_index("orb")
    other_spin = 1 - spin_index
    pick = lambda array, n: lax.dynamic_index_in_dim(array, n, 0, keepdims=False)
    occ_same, occ_other = pick(occ_energy, spin_index), pick(occ_energy, other_spin)
    virt_same, virt_other = pick(virt_energy, spin_index), pick(virt_energy, other_spin)
    across = [(0, 1), (1, 0)]

    own = jnp.swapaxes(integrals[0], 1, 2)
    occupied, width, nv = own.shape
    naux = metric_factor.shape[0]
    sources = pick(jnp.asarray(slice_sources(orb_count)), orbit_index)
    factor = jnp.take(metric_factor.reshape(orb_count, width, naux), sources, axis=0)
    factor = factor.reshape(naux, naux).T

    slices = []
    for part in gather_slices(own, orb_count):
        slices += [part] if part.ndim == 3 else [part[n] for n in range(part.shape[0])]
    own_row = [pick(s, orbit_index) for s in slices]
    early = len(slices) - 6 if len(slices) > 8 else len(slices) // 2
    raw_row = jnp.concatenate(
        [
            lax.ppermute(jnp.concatenate(own_row[:early]), "spin", across),
            lax.ppermute(jnp.concatenate(own_row[early:]), "spin", across),
        ]
    )
    if width % 16:
        slices = [jnp.concatenate(slices, axis=1)]
    fitted = fit(factor, slices, 2)

    own_energy, other_energy = pick(occ_same, orbit_index), pick(occ_other, orbit_index)
    gamma_same, dens = same_spin(fitted, orbit_index[None], own_energy + occ_same, virt_same, 2)
    gamma_other, dens = opposite_spin(
        fitted, factor, raw_row, other_energy + occ_same, virt_other, virt_same, dens, 2
    )
    returned = lax.ppermute(gamma_other, "spin", across)
    gamma = gamma_same + returned
    split = dens.reshape(orb_count // 2, 2, nv // orb_count, nv) / occupied
    kept, sent = (lax.dynamic_index_in_dim(split, n, 1, False) for n in (orbit_index % 2, 1 - orbit_index % 2))
    swap = [(d, d ^ 1) for d in range(orb_count)]
    kept, arrived = reduce_rows(kept + lax.ppermute(sent, "orb", swap), orb_count, 1)
    density = kept + arrived
    return gamma[None, None], density[None]


def local(integrals, metric_factor, occ_energy, virt_energy, orb_count):
    _, count, nv, width = integrals.shape
    fits = count * nv * metric_factor.shape[0] * 2 <= 4 * 1024 * 1024 and width % 16 == 0 and count % GROUP == 0
    chosen = local_in_vmem if fits else local_streamed
    return chosen(integrals, metric_factor, occ_energy, virt_energy, orb_count)


def solution(mesh):
    return jax.shard_map(
        functools.partial(local, orb_count=mesh.shape["orb"]),
        mesh=mesh,
        in_specs=(P("spin", None, None, "orb"), P(), P(), P()),
        out_specs=(P("spin", "orb", None, None), P("spin", "orb", None)),
        check_vma=False,
    )
```

```python
import functools

import jax
import jax.numpy as jnp
import numpy as np
from jax import lax
from jax.experimental import pallas as pl
from jax.experimental.pallas import tpu as pltpu
from jax.sharding import PartitionSpec as P

VMEM_LIMIT = 20 * 1024 * 1024
GROUP = 4
PIECES = 1
NN = (((1,), (0,)), ((), ()))
NT = (((1,), (1,)), ((), ()))
TN = (((0,), (0,)), ((), ()))


def dot(left, right, dims):
    return lax.dot_general(left, right, dims, preferred_element_type=jnp.float32)


def chip_ring(orb_count):
    chips = orb_count // 2
    order = list(range(0, chips, 2)) + list(range(chips - 1 - chips % 2, 0, -2))
    following = {order[r]: order[(r + 1) % chips] for r in range(chips)}
    return order, following


def ring_moves(orb_count):
    _, following = chip_ring(orb_count)
    forward = [(2 * p, 2 * q) for p, q in following.items()]
    backward = [(2 * q + 1, 2 * p + 1) for p, q in following.items()]
    return forward + backward


def slice_sources(orb_count):
    order, _ = chip_ring(orb_count)
    chips = len(order)
    place = {chip: r for r, chip in enumerate(order)}
    table = []
    for device in range(orb_count):
        chip, core = device // 2, device % 2
        sources = [device, device ^ 1]
        for step in range(1, chips // 2 + 1):
            ahead = order[(place[chip] + (step if core else -step)) % chips]
            behind = order[(place[chip] - (step if core else -step)) % chips]
            if 2 * step == chips:
                sources += [2 * ahead + core, 2 * behind + 1 - core]
            else:
                sources += [2 * ahead + core, 2 * ahead + 1 - core]
                sources += [2 * behind + 1 - core, 2 * behind + core]
        table.append(sources)
    return np.asarray(table, np.int32)


def gather_slices(own, orb_count):
    moves = ring_moves(orb_count)
    swap = [(d, d ^ 1) for d in range(orb_count)]
    chips = orb_count // 2
    lanes = [own, lax.ppermute(own, "orb", swap)]
    gathered = list(lanes)
    for step in range(1, chips // 2 + 1):
        if 2 * step == chips:
            lanes = lanes[:1]
        lanes = [lax.ppermute(lane, "orb", moves) for lane in lanes]
        swapped = lax.ppermute(jnp.stack(lanes), "orb", swap)
        gathered += lanes + [swapped]
    return gathered


def pieces(refs, orbital):
    for ref in refs:
        if len(ref.shape) == 3:
            yield ref[orbital]
        else:
            for lane in range(ref.shape[0]):
                yield ref[lane, orbital]


def order_factor(factor_ref, rows, orb_count):
    own = lax.axis_index("orb")
    chips, width = orb_count // 2, factor_ref.shape[0] // orb_count
    chip, core = own // 2, own % 2
    place = jnp.where(chip % 2 == 0, chip // 2, chips - (chip + 1) // 2)

    def chip_at(distance):
        there = (place + chips + jnp.where(core == 0, -distance, distance)) % chips
        return jnp.where(2 * there < chips, 2 * there, 2 * (chips - there) - 1)

    sources, first = [own ^ 1], []
    for step in range(1, chips // 2 + 1):
        ahead, behind = 2 * chip_at(step), 2 * chip_at(-step)
        back = [own] if step == 1 else []
        if 2 * step == chips:
            sources += [ahead + core, behind + 1 - core]
        elif step < chips // 2 - 1:
            sources += [ahead + core, ahead + 1 - core]
            first += [behind + 1 - core, behind + core] + back
        else:
            sources += first + [ahead + core, ahead + 1 - core, behind + 1 - core, behind + core] + back
            first = []
    for n, source in enumerate(sources):
        rows[n * width : (n + 1) * width] = factor_ref[pl.ds(pl.multiple_of(source * width, width), width)]
    return rows[...].T


def row_kernel(*refs):
    *slices, out_ref = refs
    out_ref[...] = jnp.concatenate(list(pieces(slices, lax.axis_index("orb"))), axis=0)


def stack_kernel(lanes, *refs):
    for n in range(lanes):
        refs[-1][n] = refs[n][...]


def energy_sums(virt_ref, left_spin, right_spin):
    nv = virt_ref.shape[1]
    left = jnp.broadcast_to(virt_ref[pl.ds(left_spin, 1)], (nv, nv)).T
    return left + virt_ref[pl.ds(right_spin, 1)]


def pair_energies(occ_ref, left_spin, right_spin, own):
    left = occ_ref[pl.ds(left_spin, 1)]
    chosen = lax.broadcasted_iota(jnp.int32, left.shape, 1) == own
    return jnp.sum(jnp.where(chosen, left, 0.0), axis=1, keepdims=True) + occ_ref[pl.ds(right_spin, 1)]


def amplitudes(coupling, occupied_pair, virtual_pair):
    return (coupling / (occupied_pair - virtual_pair)).astype(jnp.bfloat16)


def fit_same_kernel(orb_count, occ_ref, virt_ref, given_ref, *refs):
    slices, (factor_ref, fitted_ref, amp_ref, dens_ref) = refs[:-7], refs[-7:-3]
    rows, left, sums = refs[-3:]
    factor_ref[...] = order_factor(given_ref, rows, orb_count)
    spin, own = lax.axis_index("spin"), lax.axis_index("orb")
    count, nv = occ_ref.shape[1], virt_ref.shape[1]
    sums[...] = energy_sums(virt_ref, spin, spin)
    energies = pair_energies(occ_ref, spin, spin, own)
    raw = jnp.concatenate(list(pieces(slices, own)), axis=0)
    left[...] = dot(factor_ref[...], raw, NN).T.astype(left.dtype)
    total = None
    for start in range(0, count, GROUP):
        members = range(start, start + GROUP)
        raw = [jnp.concatenate(list(pieces(slices, j)), axis=0) for j in members]
        fitted = dot(factor_ref[...], jnp.concatenate(raw, axis=1), NN).astype(fitted_ref.dtype)
        columns = slice(start * nv, (start + GROUP) * nv)
        fitted_ref[:, columns] = fitted
        couplings = dot(left[...], fitted, NN)
        amps = []
        for n, j in enumerate(members):
            coupling = couplings[:, n * nv : (n + 1) * nv]
            amps.append(amplitudes(coupling - coupling.T, energies[:, j : j + 1], sums[...]))
        amps = jnp.concatenate(amps, axis=1)
        amp_ref[:, columns] = amps
        term = dot(amps, amps, NT)
        total = term if total is None else total + term
    dens_ref[...] = 0.5 * total


def opposite_all_kernel(
    occ_ref, virt_ref, factor_ref, early_ref, late_ref, fitted_ref, dens_in,
    amp_ref, kept_ref, sent_ref, left, sums, dens,
):
    spin, own = lax.axis_index("spin"), lax.axis_index("orb")
    count, nv = occ_ref.shape[1], virt_ref.shape[1]
    sums[...] = energy_sums(virt_ref, 1 - spin, spin)
    energies = pair_energies(occ_ref, 1 - spin, spin, own)
    raw = jnp.concatenate([early_ref[...], late_ref[...]], axis=0)
    left[...] = dot(factor_ref[...], raw, NN).T.astype(left.dtype)
    total = dens_in[...]
    for start in range(0, count, GROUP):
        columns = slice(start * nv, (start + GROUP) * nv)
        couplings = dot(left[...], fitted_ref[:, columns], NN)
        amps = []
        for n in range(GROUP):
            energy = energies[:, start + n : start + n + 1]
            amps.append(amplitudes(couplings[:, n * nv : (n + 1) * nv], energy, sums[...]))
        amp_ref[:, columns] = jnp.concatenate(amps, axis=1)
        stacked = jnp.concatenate(amps, axis=0)
        total = total + dot(stacked, stacked, TN)
    dens[...] = total / count
    core = own % 2
    chips, rows, _ = kept_ref.shape
    for chip in range(chips):
        for ref, lane in ((kept_ref, core), (sent_ref, 1 - core)):
            first = pl.multiple_of((2 * chip + lane) * rows, rows)
            ref[chip] = dens[pl.ds(first, rows)]


def gamma_kernel(amp_ref, fitted_ref, *out_refs):
    rows = out_refs[0].shape[0]
    gamma = dot(amp_ref[...], fitted_ref[...], NT)
    for n, ref in enumerate(out_refs):
        ref[...] = gamma[n * rows : (n + 1) * rows].astype(ref.dtype)


def split_kernel(bit, kept_in, arrived, *refs):
    kept_ref, sent_ref, total = refs[-3:]
    total[...] = kept_in[...] + arrived[...]
    mine = (lax.axis_index("orb") >> bit) & 1
    for n in range(kept_ref.shape[0]):
        kept_ref[n] = total[2 * n + mine]
        sent_ref[n] = total[2 * n + 1 - mine]


def finish_kernel(kept_in, arrived, gamma_in, *refs):
    *returned, gamma_ref, density_ref = refs
    rows = returned[0].shape[0]
    for n, ref in enumerate(returned):
        part = slice(n * rows, (n + 1) * rows)
        gamma_ref[part] = gamma_in[part] + ref[...].astype(jnp.float32)
    density_ref[...] = kept_in[...] + arrived[...]


def vmem_call(kernel, name, operands, outs, scratch=(), flops=0, in_hbm=0, pin=True):
    vmem, hbm = pl.BlockSpec(memory_space=pltpu.VMEM), pl.BlockSpec(memory_space=pltpu.HBM)
    moved = sum(a.size * a.dtype.itemsize for a in operands)
    if pin:
        places = [pltpu.HBM] * in_hbm + [pltpu.VMEM] * (len(operands) - in_hbm)
        operands = [pltpu.with_memory_space_constraint(*pair) for pair in zip(operands, places)]
    return pl.pallas_call(
        kernel,
        in_specs=[hbm] * in_hbm + [vmem] * (len(operands) - in_hbm),
        out_specs=[vmem] * len(outs),
        out_shape=[pltpu.VMEM(*out) if pin else jax.ShapeDtypeStruct(*out) for out in outs],
        scratch_shapes=[pltpu.VMEM(*s) if isinstance(s, tuple) else s for s in scratch],
        compiler_params=pltpu.CompilerParams(vmem_limit_bytes=VMEM_LIMIT),
        cost_estimate=pl.CostEstimate(flops=flops, bytes_accessed=moved, transcendentals=0),
        name=name,
    )(*operands)


def local_in_vmem(integrals, metric_factor, occ_energy, virt_energy, orb_count):
    across = [(0, 1), (1, 0)]
    swap = [(d, d ^ 1) for d in range(orb_count)]
    moves = ring_moves(orb_count)
    own = jnp.swapaxes(integrals[0], 1, 2)
    count, width, nv = own.shape
    naux = metric_factor.shape[0]
    half, full = jnp.bfloat16, jnp.float32
    depth = lambda part: width * sum(1 if s.ndim == 3 else s.shape[0] for s in part)

    steps = orb_count // 4
    lanes = [own, lax.ppermute(own, "orb", swap)]
    slices, swapped, early_row = lanes[1:], [], None
    for step in range(1, steps + 1):
        back = lanes[1:] if step == 1 else []
        lanes = [lax.ppermute(lane, "orb", moves) for lane in (lanes if step < steps else lanes[:1])]
        slices += lanes
        if step == steps - 2:
            sent = len(slices)
            (row,) = vmem_call(row_kernel, "early_row", slices, [((depth(slices), nv), half)])
            early_row = lax.ppermute(row, "spin", across)
        order = [early_row] if step == steps - 1 else []
        (stacked,) = vmem_call(
            functools.partial(stack_kernel, len(lanes + back)), "stack", lanes + back + order,
            [((len(lanes + back),) + own.shape, half)],
        )
        swapped.append(lax.ppermute(stacked, "orb", swap))
        if step >= steps - 2:
            slices += swapped
            swapped = []
    (row,) = vmem_call(row_kernel, "late_row", slices[sent:], [((depth(slices[sent:]), nv), half)])
    late_row = lax.ppermute(row, "spin", across)
    pair = 2 * count * nv * nv
    factor, fitted, amp_same, dens_same = vmem_call(
        functools.partial(fit_same_kernel, orb_count), "fit_same",
        [occ_energy, virt_energy, metric_factor] + slices,
        [((naux, naux), half), ((naux, count * nv), half), ((nv, count * nv), half), ((nv, nv), full)],
        [((naux, naux), half), ((nv, naux), half), ((nv, nv), full)],
    )
    rows = nv // orb_count
    amp_other, kept, sent = vmem_call(
        opposite_all_kernel, "opposite",
        [occ_energy, virt_energy, factor, early_row, late_row, fitted, dens_same],
        [((nv, count * nv), half)] + [((orb_count // 2, rows, nv), full)] * 2,
        [((nv, naux), half), ((nv, nv), full), ((nv, nv), full)],
        flops=pair * (naux + nv),
    )
    gamma_other = vmem_call(
        gamma_kernel, "gamma_other", [amp_other, fitted], [((nv // PIECES, naux), half)] * PIECES,
        flops=pair * naux,
    )
    (gamma_same,) = vmem_call(
        gamma_kernel, "gamma_same", [amp_same, fitted], [((nv, naux), full)], flops=2*pair*naux
    )
    returned = [lax.ppermute(piece, "spin", across) for piece in gamma_other]
    for bit in range(1, orb_count.bit_length() - 1):
        arrived = lax.ppermute(sent, "orb", [(d, d ^ (1 << bit - 1)) for d in range(orb_count)])
        left = orb_count >> bit + 1
        order = returned[:0] if left == 1 else []
        kept, sent = vmem_call(
            functools.partial(split_kernel, bit), "split", [kept, arrived] + order,
            [((left, rows, nv), full)] * 2, [((2 * left, rows, nv), full)],
        )
    arrived = lax.ppermute(sent, "orb", [(d, d ^ (orb_count >> 1)) for d in range(orb_count)])
    gamma, density = vmem_call(
        finish_kernel, "finish", [kept, arrived, gamma_same] + returned,
        [((nv, naux), full), ((1, rows, nv), full)], pin=False,
    )
    return gamma[None, None], density


def fit_kernel(factor_ref, *refs):
    slices, out_ref = refs[:-1], refs[-1]
    for g in range(out_ref.shape[0]):
        raw = jnp.concatenate([piece[g] for piece in slices], axis=0)
        out_ref[g] = dot(factor_ref[...], raw, NN).astype(out_ref.dtype)


def fit(factor, slices, group):
    count, _, virt = slices[0].shape
    naux = factor.shape[0]
    return pl.pallas_call(
        fit_kernel,
        grid=(count // group,),
        in_specs=[pl.BlockSpec(factor.shape, lambda j: (0, 0))]
        + [pl.BlockSpec((group,) + s.shape[1:], lambda j: (j, 0, 0)) for s in slices],
        out_specs=pl.BlockSpec((group, naux, virt), lambda j: (j, 0, 0)),
        out_shape=jax.ShapeDtypeStruct((count, naux, virt), jnp.bfloat16),
        compiler_params=pltpu.CompilerParams(vmem_limit_bytes=VMEM_LIMIT),
        name="fit",
    )(factor, *slices)


def same_kernel(own_ref, pair_ref, own_block, blocks, v_col, v_row, gamma_ref, dens_ref, left):
    step = pl.program_id(0)

    @pl.when(step == 0)
    def _():
        left[...] = own_block[0].T
        gamma_ref[...] = jnp.zeros_like(gamma_ref)
        dens_ref[...] = jnp.zeros_like(dens_ref)

    group = blocks.shape[0]
    for g in range(group):
        right = blocks[g]
        coupling = dot(left[...], right, NN)
        coupling = coupling - coupling.T
        denominator = (pair_ref[step * group + g] - v_col[...]) - v_row[...]
        amplitude = (coupling / denominator).astype(jnp.bfloat16)
        gamma_ref[...] += dot(amplitude, right, NT)
        dens_ref[...] += 0.5 * dot(amplitude, amplitude, NT)


def same_spin(fitted, own_index, pair_energy, virt, group):
    count, naux, nv = fitted.shape
    whole = lambda shape: pl.BlockSpec(shape, lambda j, *_: (0,) * len(shape))
    return pl.pallas_call(
        same_kernel,
        grid_spec=pltpu.PrefetchScalarGridSpec(
            num_scalar_prefetch=2,
            grid=(count // group,),
            in_specs=[
                pl.BlockSpec((1, naux, nv), lambda j, own, pair: (own[0], 0, 0)),
                pl.BlockSpec((group, naux, nv), lambda j, own, pair: (j, 0, 0)),
                whole((nv, 1)),
                whole((1, nv)),
            ],
            out_specs=[whole((nv, naux)), whole((nv, nv))],
            scratch_shapes=[pltpu.VMEM((nv, naux), jnp.bfloat16)],
        ),
        out_shape=[
            jax.ShapeDtypeStruct((nv, naux), jnp.float32),
            jax.ShapeDtypeStruct((nv, nv), jnp.float32),
        ],
        compiler_params=pltpu.CompilerParams(vmem_limit_bytes=VMEM_LIMIT),
        name="same_spin",
    )(own_index, pair_energy, fitted, fitted, virt[:, None], virt[None, :])


def opposite_kernel(pair_ref, factor, raw, blocks, v_col, v_row, dens_in, gamma_ref, dens_ref, left):
    step = pl.program_id(0)

    @pl.when(step == 0)
    def _():
        left[...] = dot(factor[...], raw[...], NN).astype(left.dtype).T
        gamma_ref[...] = jnp.zeros_like(gamma_ref)
        dens_ref[...] = dens_in[...]

    group = blocks.shape[0]
    for g in range(group):
        right = blocks[g]
        coupling = dot(left[...], right, NN)
        denominator = (pair_ref[step * group + g] - v_col[...]) - v_row[...]
        amplitude = (coupling / denominator).astype(jnp.bfloat16)
        gamma_ref[...] += dot(amplitude, right, NT)
        dens_ref[...] += dot(amplitude, amplitude, TN)


def opposite_spin(fitted, factor, raw, pair_energy, virt_left, virt_right, dens, group):
    count, naux, nv = fitted.shape
    whole = lambda shape: pl.BlockSpec(shape, lambda j, *_: (0,) * len(shape))
    return pl.pallas_call(
        opposite_kernel,
        grid_spec=pltpu.PrefetchScalarGridSpec(
            num_scalar_prefetch=1,
            grid=(count // group,),
            in_specs=[
                whole(factor.shape),
                whole(raw.shape),
                pl.BlockSpec((group, naux, nv), lambda j, pair: (j, 0, 0)),
                whole((nv, 1)),
                whole((1, nv)),
                whole((nv, nv)),
            ],
            out_specs=[whole((nv, naux)), whole((nv, nv))],
            scratch_shapes=[pltpu.VMEM((nv, naux), jnp.bfloat16)],
        ),
        out_shape=[
            jax.ShapeDtypeStruct((nv, naux), jnp.float32),
            jax.ShapeDtypeStruct((nv, nv), jnp.float32),
        ],
        compiler_params=pltpu.CompilerParams(vmem_limit_bytes=VMEM_LIMIT),
        name="opposite_spin",
    )(pair_energy, factor, raw, fitted, virt_left[:, None], virt_right[None, :], dens)


def reduce_rows(total, orb_count, keep):
    index = lax.axis_index("orb")
    bits = orb_count.bit_length() - 1
    rows = total.reshape((2,) * (bits - 1) + total.shape[1:])
    for bit in range(1, bits + 1 - keep.bit_length()):
        axis = bits - 1 - bit
        mine = (index >> bit) & 1
        moves = [(d, d ^ (1 << bit)) for d in range(orb_count)]
        kept = lax.dynamic_index_in_dim(rows, mine, axis, keepdims=False)
        sent = lax.dynamic_index_in_dim(rows, 1 - mine, axis, keepdims=False)
        arrived = lax.ppermute(sent, "orb", moves)
        rows = kept + arrived
    return kept, arrived


def local_streamed(integrals, metric_factor, occ_energy, virt_energy, orb_count):
    spin_index = lax.axis_index("spin")
    orbit_index = lax.axis_index("orb")
    other_spin = 1 - spin_index
    pick = lambda array, n: lax.dynamic_index_in_dim(array, n, 0, keepdims=False)
    occ_same, occ_other = pick(occ_energy, spin_index), pick(occ_energy, other_spin)
    virt_same, virt_other = pick(virt_energy, spin_index), pick(virt_energy, other_spin)
    across = [(0, 1), (1, 0)]

    own = jnp.swapaxes(integrals[0], 1, 2)
    occupied, width, nv = own.shape
    naux = metric_factor.shape[0]
    sources = pick(jnp.asarray(slice_sources(orb_count)), orbit_index)
    factor = jnp.take(metric_factor.reshape(orb_count, width, naux), sources, axis=0)
    factor = factor.reshape(naux, naux).T

    slices = []
    for part in gather_slices(own, orb_count):
        slices += [part] if part.ndim == 3 else [part[n] for n in range(part.shape[0])]
    own_row = [pick(s, orbit_index) for s in slices]
    early = len(slices) - 6 if len(slices) > 8 else len(slices) // 2
    raw_row = jnp.concatenate(
        [
            lax.ppermute(jnp.concatenate(own_row[:early]), "spin", across),
            lax.ppermute(jnp.concatenate(own_row[early:]), "spin", across),
        ]
    )
    if width % 16:
        slices = [jnp.concatenate(slices, axis=1)]
    fitted = fit(factor, slices, 2)

    own_energy, other_energy = pick(occ_same, orbit_index), pick(occ_other, orbit_index)
    gamma_same, dens = same_spin(fitted, orbit_index[None], own_energy + occ_same, virt_same, 2)
    gamma_other, dens = opposite_spin(
        fitted, factor, raw_row, other_energy + occ_same, virt_other, virt_same, dens, 2
    )
    returned = lax.ppermute(gamma_other, "spin", across)
    gamma = gamma_same + returned
    split = dens.reshape(orb_count // 2, 2, nv // orb_count, nv) / occupied
    kept, sent = (lax.dynamic_index_in_dim(split, n, 1, False) for n in (orbit_index % 2, 1 - orbit_index % 2))
    swap = [(d, d ^ 1) for d in range(orb_count)]
    kept, arrived = reduce_rows(kept + lax.ppermute(sent, "orb", swap), orb_count, 1)
    density = kept + arrived
    return gamma[None, None], density[None]


def local(integrals, metric_factor, occ_energy, virt_energy, orb_count):
    _, count, nv, width = integrals.shape
    fits = count * nv * metric_factor.shape[0] * 2 <= 4 * 1024 * 1024 and width % 16 == 0 and count % GROUP == 0
    chosen = local_in_vmem if fits else local_streamed
    return chosen(integrals, metric_factor, occ_energy, virt_energy, orb_count)


def solution(mesh):
    return jax.shard_map(
        functools.partial(local, orb_count=mesh.shape["orb"]),
        mesh=mesh,
        in_specs=(P("spin", None, None, "orb"), P(), P(), P()),
        out_specs=(P("spin", "orb", None, None), P("spin", "orb", None)),
        check_vma=False,
    )
```

```python
import functools

import jax
import jax.numpy as jnp
import numpy as np
from jax import lax
from jax.experimental import pallas as pl
from jax.experimental.pallas import tpu as pltpu
from jax.sharding import PartitionSpec as P

VMEM_LIMIT = 20 * 1024 * 1024
GROUP = 4
PIECES = 1
NN = (((1,), (0,)), ((), ()))
NT = (((1,), (1,)), ((), ()))
TN = (((0,), (0,)), ((), ()))


def dot(left, right, dims):
    return lax.dot_general(left, right, dims, preferred_element_type=jnp.float32)


def chip_ring(orb_count):
    chips = orb_count // 2
    order = list(range(0, chips, 2)) + list(range(chips - 1 - chips % 2, 0, -2))
    following = {order[r]: order[(r + 1) % chips] for r in range(chips)}
    return order, following


def ring_moves(orb_count):
    _, following = chip_ring(orb_count)
    forward = [(2 * p, 2 * q) for p, q in following.items()]
    backward = [(2 * q + 1, 2 * p + 1) for p, q in following.items()]
    return forward + backward


def slice_sources(orb_count):
    order, _ = chip_ring(orb_count)
    chips = len(order)
    place = {chip: r for r, chip in enumerate(order)}
    table = []
    for device in range(orb_count):
        chip, core = device // 2, device % 2
        sources = [device, device ^ 1]
        for step in range(1, chips // 2 + 1):
            ahead = order[(place[chip] + (step if core else -step)) % chips]
            behind = order[(place[chip] - (step if core else -step)) % chips]
            if 2 * step == chips:
                sources += [2 * ahead + core, 2 * behind + 1 - core]
            else:
                sources += [2 * ahead + core, 2 * ahead + 1 - core]
                sources += [2 * behind + 1 - core, 2 * behind + core]
        table.append(sources)
    return np.asarray(table, np.int32)


def gather_slices(own, orb_count):
    moves = ring_moves(orb_count)
    swap = [(d, d ^ 1) for d in range(orb_count)]
    chips = orb_count // 2
    lanes = [own, lax.ppermute(own, "orb", swap)]
    gathered = list(lanes)
    for step in range(1, chips // 2 + 1):
        if 2 * step == chips:
            lanes = lanes[:1]
        lanes = [lax.ppermute(lane, "orb", moves) for lane in lanes]
        swapped = lax.ppermute(jnp.stack(lanes), "orb", swap)
        gathered += lanes + [swapped]
    return gathered


def pieces(refs, orbital):
    for ref in refs:
        if len(ref.shape) == 3:
            yield ref[orbital]
        else:
            for lane in range(ref.shape[0]):
                yield ref[lane, orbital]


def order_factor(factor_ref, rows, orb_count):
    own = lax.axis_index("orb")
    chips, width = orb_count // 2, factor_ref.shape[0] // orb_count
    chip, core = own // 2, own % 2
    place = jnp.where(chip % 2 == 0, chip // 2, chips - (chip + 1) // 2)

    def chip_at(distance):
        there = (place + chips + jnp.where(core == 0, -distance, distance)) % chips
        return jnp.where(2 * there < chips, 2 * there, 2 * (chips - there) - 1)

    sources, first = [own ^ 1], []
    for step in range(1, chips // 2 + 1):
        ahead, behind = 2 * chip_at(step), 2 * chip_at(-step)
        back = [own] if step == 1 else []
        if 2 * step == chips:
            sources += [ahead + core, behind + 1 - core]
        elif step < chips // 2 - 1:
            sources += [ahead + core, ahead + 1 - core]
            first += [behind + 1 - core, behind + core] + back
        else:
            sources += first + [ahead + core, ahead + 1 - core, behind + 1 - core, behind + core] + back
            first = []
    for n, source in enumerate(sources):
        rows[n * width : (n + 1) * width] = factor_ref[pl.ds(pl.multiple_of(source * width, width), width)]
    return rows[...].T


def row_kernel(*refs):
    *slices, out_ref = refs
    out_ref[...] = jnp.concatenate(list(pieces(slices, lax.axis_index("orb"))), axis=0)


def stack_kernel(lanes, *refs):
    for n in range(lanes):
        refs[-1][n] = refs[n][...]


def energy_sums(virt_ref, left_spin, right_spin):
    nv = virt_ref.shape[1]
    left = jnp.broadcast_to(virt_ref[pl.ds(left_spin, 1)], (nv, nv)).T
    return left + virt_ref[pl.ds(right_spin, 1)]


def pair_energies(occ_ref, left_spin, right_spin, own):
    left = occ_ref[pl.ds(left_spin, 1)]
    chosen = lax.broadcasted_iota(jnp.int32, left.shape, 1) == own
    return jnp.sum(jnp.where(chosen, left, 0.0), axis=1, keepdims=True) + occ_ref[pl.ds(right_spin, 1)]


def amplitudes(coupling, occupied_pair, virtual_pair):
    return (coupling / (occupied_pair - virtual_pair)).astype(jnp.bfloat16)


def early_fit_kernel(orb_count, given_ref, *refs):
    *slices, factor_ref, early_ref, rows = refs
    factor_ref[...] = order_factor(given_ref, rows, orb_count)
    nv = early_ref.shape[1] // orb_count
    depth = early_depth(slices)
    for start in range(0, orb_count, GROUP):
        raw = [jnp.concatenate(list(pieces(slices, j)), axis=0) for j in range(start, start + GROUP)]
        columns = slice(start * nv, (start + GROUP) * nv)
        early_ref[:, columns] = dot(factor_ref[:, :depth], jnp.concatenate(raw, axis=1), NN)


def early_depth(slices):
    return sum(s.shape[-2] * (1 if len(s.shape) == 3 else s.shape[0]) for s in slices)


def fit_same_kernel(occ_ref, virt_ref, factor_ref, early_ref, *refs):
    slices, (fitted_ref, amp_ref, dens_ref, left, sums) = refs[:-5], refs[-5:]
    first = factor_ref.shape[0] - early_depth(slices)
    spin, own = lax.axis_index("spin"), lax.axis_index("orb")
    count, nv = occ_ref.shape[1], virt_ref.shape[1]
    sums[...] = energy_sums(virt_ref, spin, spin)
    energies = pair_energies(occ_ref, spin, spin, own)
    raw = jnp.concatenate(list(pieces(slices, own)), axis=0)
    early = early_ref[:, pl.ds(pl.multiple_of(own * nv, nv), nv)]
    left[...] = (early + dot(factor_ref[:, first:], raw, NN)).T.astype(left.dtype)
    total = None
    for start in range(0, count, GROUP):
        members = range(start, start + GROUP)
        raw = [jnp.concatenate(list(pieces(slices, j)), axis=0) for j in members]
        columns = slice(start * nv, (start + GROUP) * nv)
        late = dot(factor_ref[:, first:], jnp.concatenate(raw, axis=1), NN)
        fitted = (early_ref[:, columns] + late).astype(fitted_ref.dtype)
        fitted_ref[:, columns] = fitted
        couplings = dot(left[...], fitted, NN)
        amps = []
        for n, j in enumerate(members):
            coupling = couplings[:, n * nv : (n + 1) * nv]
            amps.append(amplitudes(coupling - coupling.T, energies[:, j : j + 1], sums[...]))
        amps = jnp.concatenate(amps, axis=1)
        amp_ref[:, columns] = amps
        term = dot(amps, amps, NT)
        total = term if total is None else total + term
    dens_ref[...] = 0.5 * total


def opposite_all_kernel(
    occ_ref, virt_ref, factor_ref, early_ref, late_ref, last_ref, fitted_ref, dens_in,
    amp_ref, kept_ref, sent_ref, left, sums, dens,
):
    spin, own = lax.axis_index("spin"), lax.axis_index("orb")
    count, nv = occ_ref.shape[1], virt_ref.shape[1]
    sums[...] = energy_sums(virt_ref, 1 - spin, spin)
    energies = pair_energies(occ_ref, 1 - spin, spin, own)
    raw = jnp.concatenate([early_ref[...], late_ref[...], last_ref[...]], axis=0)
    left[...] = dot(factor_ref[...], raw, NN).T.astype(left.dtype)
    total = dens_in[...]
    for start in range(0, count, GROUP):
        columns = slice(start * nv, (start + GROUP) * nv)
        couplings = dot(left[...], fitted_ref[:, columns], NN)
        amps = []
        for n in range(GROUP):
            energy = energies[:, start + n : start + n + 1]
            amps.append(amplitudes(couplings[:, n * nv : (n + 1) * nv], energy, sums[...]))
        amp_ref[:, columns] = jnp.concatenate(amps, axis=1)
        stacked = jnp.concatenate(amps, axis=0)
        total = total + dot(stacked, stacked, TN)
    dens[...] = total / count
    core = own % 2
    chips, rows, _ = kept_ref.shape
    for chip in range(chips):
        for ref, lane in ((kept_ref, core), (sent_ref, 1 - core)):
            first = pl.multiple_of((2 * chip + lane) * rows, rows)
            ref[chip] = dens[pl.ds(first, rows)]


def gamma_kernel(amp_ref, fitted_ref, *out_refs):
    rows = out_refs[0].shape[0]
    gamma = dot(amp_ref[...], fitted_ref[...], NT)
    for n, ref in enumerate(out_refs):
        ref[...] = gamma[n * rows : (n + 1) * rows].astype(ref.dtype)


def split_kernel(bit, kept_in, arrived, *refs):
    kept_ref, sent_ref, total = refs[-3:]
    total[...] = kept_in[...] + arrived[...]
    mine = (lax.axis_index("orb") >> bit) & 1
    for n in range(kept_ref.shape[0]):
        kept_ref[n] = total[2 * n + mine]
        sent_ref[n] = total[2 * n + 1 - mine]


def finish_kernel(kept_in, arrived, gamma_in, *refs):
    *returned, gamma_ref, density_ref = refs
    rows = returned[0].shape[0]
    for n, ref in enumerate(returned):
        part = slice(n * rows, (n + 1) * rows)
        gamma_ref[part] = gamma_in[part] + ref[...].astype(jnp.float32)
    density_ref[...] = kept_in[...] + arrived[...]


def vmem_call(kernel, name, operands, outs, scratch=(), flops=0, in_hbm=0, pin=True):
    vmem, hbm = pl.BlockSpec(memory_space=pltpu.VMEM), pl.BlockSpec(memory_space=pltpu.HBM)
    moved = sum(a.size * a.dtype.itemsize for a in operands) if flops else 0
    if pin:
        places = [pltpu.HBM] * in_hbm + [pltpu.VMEM] * (len(operands) - in_hbm)
        operands = [pltpu.with_memory_space_constraint(*pair) for pair in zip(operands, places)]
    return pl.pallas_call(
        kernel,
        in_specs=[hbm] * in_hbm + [vmem] * (len(operands) - in_hbm),
        out_specs=[vmem] * len(outs),
        out_shape=[pltpu.VMEM(*out) if pin else jax.ShapeDtypeStruct(*out) for out in outs],
        scratch_shapes=[pltpu.VMEM(*s) if isinstance(s, tuple) else s for s in scratch],
        compiler_params=pltpu.CompilerParams(vmem_limit_bytes=VMEM_LIMIT),
        cost_estimate=pl.CostEstimate(flops=flops, bytes_accessed=moved, transcendentals=0),
        name=name,
    )(*operands)


def local_in_vmem(integrals, metric_factor, occ_energy, virt_energy, orb_count):
    across = [(0, 1), (1, 0)]
    swap = [(d, d ^ 1) for d in range(orb_count)]
    moves = ring_moves(orb_count)
    own = jnp.swapaxes(integrals[0], 1, 2)
    count, width, nv = own.shape
    naux = metric_factor.shape[0]
    half, full = jnp.bfloat16, jnp.float32
    depth = lambda part: width * sum(1 if s.ndim == 3 else s.shape[0] for s in part)

    pair = 2 * count * nv * nv
    steps = orb_count // 4
    lanes = [own, lax.ppermute(own, "orb", swap)]
    slices, swapped, early_row = lanes[1:], [], None
    for step in range(1, steps + 1):
        back = lanes[1:] if step == 1 else []
        lanes = [lax.ppermute(lane, "orb", moves) for lane in (lanes if step < steps else lanes[:1])]
        slices += lanes
        if step == steps - 2:
            sent = len(slices)
            (row,) = vmem_call(row_kernel, "early_row", slices, [((depth(slices), nv), half)])
            early_row = lax.ppermute(row, "spin", across)
        if step == steps - 1:
            factor, early = vmem_call(
                functools.partial(early_fit_kernel, orb_count), "early_fit", [metric_factor] + slices[: sent + 1],
                [((naux, naux), half), ((naux, count * nv), full)], [((naux, naux), half)], flops=0,
            )
        order = [early_row] if step == steps - 1 else [early] if step == steps else []
        (stacked,) = vmem_call(
            functools.partial(stack_kernel, len(lanes + back)), "stack", lanes + back + order,
            [((len(lanes + back),) + own.shape, half)],
        )
        swapped.append(lax.ppermute(stacked, "orb", swap))
        if step >= steps - 2:
            slices += swapped
            swapped = []
    rows_sent, cut = [early_row], sent+4
    for part in (slices[sent:cut], slices[cut:]):
        (row,) = vmem_call(row_kernel, "late_row", part, [((depth(part), nv), half)])
        rows_sent.append(lax.ppermute(row, "spin", across))
    fitted, amp_same, dens_same = vmem_call(
        fit_same_kernel, "fit_same", [occ_energy, virt_energy, factor, early] + slices[sent + 1 :],
        [((naux, count * nv), half), ((nv, count * nv), half), ((nv, nv), full)],
        [((nv, naux), half), ((nv, nv), full)],
    )
    rows = nv // orb_count
    amp_other, kept, sent = vmem_call(
        opposite_all_kernel, "opposite",
        [occ_energy, virt_energy, factor] + rows_sent + [fitted, dens_same],
        [((nv, count * nv), half)] + [((orb_count // 2, rows, nv), full)] * 2,
        [((nv, naux), half), ((nv, nv), full), ((nv, nv), full)],
        flops=pair * (naux + nv),
    )
    gamma_other = vmem_call(
        gamma_kernel, "gamma_other", [amp_other, fitted], [((nv // PIECES, naux), half)] * PIECES,
        flops=pair * naux,
    )
    (gamma_same,) = vmem_call(
        gamma_kernel, "gamma_same", [amp_same, fitted], [((nv, naux), full)], flops=2*pair*naux
    )
    returned = [lax.ppermute(piece, "spin", across) for piece in gamma_other]
    for bit in range(1, orb_count.bit_length() - 1):
        arrived = lax.ppermute(sent, "orb", [(d, d ^ (1 << bit - 1)) for d in range(orb_count)])
        left = orb_count >> bit + 1
        order = returned[:0] if left == 1 else []
        kept, sent = vmem_call(
            functools.partial(split_kernel, bit), "split", [kept, arrived] + order,
            [((left, rows, nv), full)] * 2, [((2 * left, rows, nv), full)],
        )
    arrived = lax.ppermute(sent, "orb", [(d, d ^ (orb_count >> 1)) for d in range(orb_count)])
    gamma, density = vmem_call(
        finish_kernel, "finish", [kept, arrived, gamma_same] + returned,
        [((nv, naux), full), ((1, rows, nv), full)], pin=False,
    )
    return gamma[None, None], density


def fit_kernel(factor_ref, *refs):
    slices, out_ref = refs[:-1], refs[-1]
    for g in range(out_ref.shape[0]):
        raw = jnp.concatenate([piece[g] for piece in slices], axis=0)
        out_ref[g] = dot(factor_ref[...], raw, NN).astype(out_ref.dtype)


def fit(factor, slices, group):
    count, _, virt = slices[0].shape
    naux = factor.shape[0]
    return pl.pallas_call(
        fit_kernel,
        grid=(count // group,),
        in_specs=[pl.BlockSpec(factor.shape, lambda j: (0, 0))]
        + [pl.BlockSpec((group,) + s.shape[1:], lambda j: (j, 0, 0)) for s in slices],
        out_specs=pl.BlockSpec((group, naux, virt), lambda j: (j, 0, 0)),
        out_shape=jax.ShapeDtypeStruct((count, naux, virt), jnp.bfloat16),
        compiler_params=pltpu.CompilerParams(vmem_limit_bytes=VMEM_LIMIT),
        name="fit",
    )(factor, *slices)


def same_kernel(own_ref, pair_ref, own_block, blocks, v_col, v_row, gamma_ref, dens_ref, left):
    step = pl.program_id(0)

    @pl.when(step == 0)
    def _():
        left[...] = own_block[0].T
        gamma_ref[...] = jnp.zeros_like(gamma_ref)
        dens_ref[...] = jnp.zeros_like(dens_ref)

    group = blocks.shape[0]
    for g in range(group):
        right = blocks[g]
        coupling = dot(left[...], right, NN)
        coupling = coupling - coupling.T
        denominator = (pair_ref[step * group + g] - v_col[...]) - v_row[...]
        amplitude = (coupling / denominator).astype(jnp.bfloat16)
        gamma_ref[...] += dot(amplitude, right, NT)
        dens_ref[...] += 0.5 * dot(amplitude, amplitude, NT)


def same_spin(fitted, own_index, pair_energy, virt, group):
    count, naux, nv = fitted.shape
    whole = lambda shape: pl.BlockSpec(shape, lambda j, *_: (0,) * len(shape))
    return pl.pallas_call(
        same_kernel,
        grid_spec=pltpu.PrefetchScalarGridSpec(
            num_scalar_prefetch=2,
            grid=(count // group,),
            in_specs=[
                pl.BlockSpec((1, naux, nv), lambda j, own, pair: (own[0], 0, 0)),
                pl.BlockSpec((group, naux, nv), lambda j, own, pair: (j, 0, 0)),
                whole((nv, 1)),
                whole((1, nv)),
            ],
            out_specs=[whole((nv, naux)), whole((nv, nv))],
            scratch_shapes=[pltpu.VMEM((nv, naux), jnp.bfloat16)],
        ),
        out_shape=[
            jax.ShapeDtypeStruct((nv, naux), jnp.float32),
            jax.ShapeDtypeStruct((nv, nv), jnp.float32),
        ],
        compiler_params=pltpu.CompilerParams(vmem_limit_bytes=VMEM_LIMIT),
        name="same_spin",
    )(own_index, pair_energy, fitted, fitted, virt[:, None], virt[None, :])


def opposite_kernel(pair_ref, factor, raw, blocks, v_col, v_row, dens_in, gamma_ref, dens_ref, left):
    step = pl.program_id(0)

    @pl.when(step == 0)
    def _():
        left[...] = dot(factor[...], raw[...], NN).astype(left.dtype).T
        gamma_ref[...] = jnp.zeros_like(gamma_ref)
        dens_ref[...] = dens_in[...]

    group = blocks.shape[0]
    for g in range(group):
        right = blocks[g]
        coupling = dot(left[...], right, NN)
        denominator = (pair_ref[step * group + g] - v_col[...]) - v_row[...]
        amplitude = (coupling / denominator).astype(jnp.bfloat16)
        gamma_ref[...] += dot(amplitude, right, NT)
        dens_ref[...] += dot(amplitude, amplitude, TN)


def opposite_spin(fitted, factor, raw, pair_energy, virt_left, virt_right, dens, group):
    count, naux, nv = fitted.shape
    whole = lambda shape: pl.BlockSpec(shape, lambda j, *_: (0,) * len(shape))
    return pl.pallas_call(
        opposite_kernel,
        grid_spec=pltpu.PrefetchScalarGridSpec(
            num_scalar_prefetch=1,
            grid=(count // group,),
            in_specs=[
                whole(factor.shape),
                whole(raw.shape),
                pl.BlockSpec((group, naux, nv), lambda j, pair: (j, 0, 0)),
                whole((nv, 1)),
                whole((1, nv)),
                whole((nv, nv)),
            ],
            out_specs=[whole((nv, naux)), whole((nv, nv))],
            scratch_shapes=[pltpu.VMEM((nv, naux), jnp.bfloat16)],
        ),
        out_shape=[
            jax.ShapeDtypeStruct((nv, naux), jnp.float32),
            jax.ShapeDtypeStruct((nv, nv), jnp.float32),
        ],
        compiler_params=pltpu.CompilerParams(vmem_limit_bytes=VMEM_LIMIT),
        name="opposite_spin",
    )(pair_energy, factor, raw, fitted, virt_left[:, None], virt_right[None, :], dens)


def reduce_rows(total, orb_count, keep):
    index = lax.axis_index("orb")
    bits = orb_count.bit_length() - 1
    rows = total.reshape((2,) * (bits - 1) + total.shape[1:])
    for bit in range(1, bits + 1 - keep.bit_length()):
        axis = bits - 1 - bit
        mine = (index >> bit) & 1
        moves = [(d, d ^ (1 << bit)) for d in range(orb_count)]
        kept = lax.dynamic_index_in_dim(rows, mine, axis, keepdims=False)
        sent = lax.dynamic_index_in_dim(rows, 1 - mine, axis, keepdims=False)
        arrived = lax.ppermute(sent, "orb", moves)
        rows = kept + arrived
    return kept, arrived


def local_streamed(integrals, metric_factor, occ_energy, virt_energy, orb_count):
    spin_index = lax.axis_index("spin")
    orbit_index = lax.axis_index("orb")
    other_spin = 1 - spin_index
    pick = lambda array, n: lax.dynamic_index_in_dim(array, n, 0, keepdims=False)
    occ_same, occ_other = pick(occ_energy, spin_index), pick(occ_energy, other_spin)
    virt_same, virt_other = pick(virt_energy, spin_index), pick(virt_energy, other_spin)
    across = [(0, 1), (1, 0)]

    own = jnp.swapaxes(integrals[0], 1, 2)
    occupied, width, nv = own.shape
    naux = metric_factor.shape[0]
    sources = pick(jnp.asarray(slice_sources(orb_count)), orbit_index)
    factor = jnp.take(metric_factor.reshape(orb_count, width, naux), sources, axis=0)
    factor = factor.reshape(naux, naux).T

    slices = []
    for part in gather_slices(own, orb_count):
        slices += [part] if part.ndim == 3 else [part[n] for n in range(part.shape[0])]
    own_row = [pick(s, orbit_index) for s in slices]
    early = len(slices) - 6 if len(slices) > 8 else len(slices) // 2
    raw_row = jnp.concatenate(
        [
            lax.ppermute(jnp.concatenate(own_row[:early]), "spin", across),
            lax.ppermute(jnp.concatenate(own_row[early:]), "spin", across),
        ]
    )
    if width % 16:
        slices = [jnp.concatenate(slices, axis=1)]
    fitted = fit(factor, slices, 2)

    own_energy, other_energy = pick(occ_same, orbit_index), pick(occ_other, orbit_index)
    gamma_same, dens = same_spin(fitted, orbit_index[None], own_energy + occ_same, virt_same, 2)
    gamma_other, dens = opposite_spin(
        fitted, factor, raw_row, other_energy + occ_same, virt_other, virt_same, dens, 2
    )
    returned = lax.ppermute(gamma_other, "spin", across)
    gamma = gamma_same + returned
    split = dens.reshape(orb_count // 2, 2, nv // orb_count, nv) / occupied
    kept, sent = (lax.dynamic_index_in_dim(split, n, 1, False) for n in (orbit_index % 2, 1 - orbit_index % 2))
    swap = [(d, d ^ 1) for d in range(orb_count)]
    kept, arrived = reduce_rows(kept + lax.ppermute(sent, "orb", swap), orb_count, 1)
    density = kept + arrived
    return gamma[None, None], density[None]


def local(integrals, metric_factor, occ_energy, virt_energy, orb_count):
    _, count, nv, width = integrals.shape
    fits = count * nv * metric_factor.shape[0] * 2 <= 4 * 1024 * 1024 and width % 16 == 0 and count % GROUP == 0
    chosen = local_in_vmem if fits else local_streamed
    return chosen(integrals, metric_factor, occ_energy, virt_energy, orb_count)


def solution(mesh):
    return jax.shard_map(
        functools.partial(local, orb_count=mesh.shape["orb"]),
        mesh=mesh,
        in_specs=(P("spin", None, None, "orb"), P(), P(), P()),
        out_specs=(P("spin", "orb", None, None), P("spin", "orb", None)),
        check_vma=False,
    )
```

```python
import functools

import jax
import jax.numpy as jnp
import numpy as np
from jax import lax
from jax.experimental import pallas as pl
from jax.experimental.pallas import tpu as pltpu
from jax.sharding import PartitionSpec as P

VMEM_LIMIT = 20 * 1024 * 1024
GROUP = 4
PIECES = 1
NN = (((1,), (0,)), ((), ()))
NT = (((1,), (1,)), ((), ()))
TN = (((0,), (0,)), ((), ()))


def dot(left, right, dims):
    return lax.dot_general(left, right, dims, preferred_element_type=jnp.float32)


def chip_ring(orb_count):
    chips = orb_count // 2
    order = list(range(0, chips, 2)) + list(range(chips - 1 - chips % 2, 0, -2))
    following = {order[r]: order[(r + 1) % chips] for r in range(chips)}
    return order, following


def ring_moves(orb_count):
    _, following = chip_ring(orb_count)
    forward = [(2 * p, 2 * q) for p, q in following.items()]
    backward = [(2 * q + 1, 2 * p + 1) for p, q in following.items()]
    return forward + backward


def slice_sources(orb_count):
    order, _ = chip_ring(orb_count)
    chips = len(order)
    place = {chip: r for r, chip in enumerate(order)}
    table = []
    for device in range(orb_count):
        chip, core = device // 2, device % 2
        sources = [device, device ^ 1]
        for step in range(1, chips // 2 + 1):
            ahead = order[(place[chip] + (step if core else -step)) % chips]
            behind = order[(place[chip] - (step if core else -step)) % chips]
            if 2 * step == chips:
                sources += [2 * ahead + core, 2 * behind + 1 - core]
            else:
                sources += [2 * ahead + core, 2 * ahead + 1 - core]
                sources += [2 * behind + 1 - core, 2 * behind + core]
        table.append(sources)
    return np.asarray(table, np.int32)


def gather_slices(own, orb_count):
    moves = ring_moves(orb_count)
    swap = [(d, d ^ 1) for d in range(orb_count)]
    chips = orb_count // 2
    lanes = [own, lax.ppermute(own, "orb", swap)]
    gathered = list(lanes)
    for step in range(1, chips // 2 + 1):
        if 2 * step == chips:
            lanes = lanes[:1]
        lanes = [lax.ppermute(lane, "orb", moves) for lane in lanes]
        swapped = lax.ppermute(jnp.stack(lanes), "orb", swap)
        gathered += lanes + [swapped]
    return gathered


def pieces(refs, orbital):
    for ref in refs:
        if len(ref.shape) == 3:
            yield ref[orbital]
        else:
            for lane in range(ref.shape[0]):
                yield ref[lane, orbital]


def order_factor(factor_ref, rows, orb_count):
    own = lax.axis_index("orb")
    chips, width = orb_count // 2, factor_ref.shape[0] // orb_count
    chip, core = own // 2, own % 2
    place = jnp.where(chip % 2 == 0, chip // 2, chips - (chip + 1) // 2)

    def chip_at(distance):
        there = (place + chips + jnp.where(core == 0, -distance, distance)) % chips
        return jnp.where(2 * there < chips, 2 * there, 2 * (chips - there) - 1)

    sources, first = [own ^ 1], []
    for step in range(1, chips // 2 + 1):
        ahead, behind = 2 * chip_at(step), 2 * chip_at(-step)
        back = [own] if step == 1 else []
        if 2 * step == chips:
            sources += [ahead + core, behind + 1 - core]
        elif step < chips // 2 - 1:
            sources += [ahead + core, ahead + 1 - core]
            first += [behind + 1 - core, behind + core] + back
        else:
            sources += first + [ahead + core, ahead + 1 - core, behind + 1 - core, behind + core] + back
            first = []
    for n, source in enumerate(sources):
        rows[n * width : (n + 1) * width] = factor_ref[pl.ds(pl.multiple_of(source * width, width), width)]
    return rows[...].T


def row_kernel(*refs):
    *slices, out_ref = refs
    out_ref[...] = jnp.concatenate(list(pieces(slices, lax.axis_index("orb"))), axis=0)


def stack_kernel(lanes, *refs):
    for n in range(lanes):
        refs[-1][n] = refs[n][...]


def energy_sums(virt_ref, left_spin, right_spin):
    nv = virt_ref.shape[1]
    left = jnp.broadcast_to(virt_ref[pl.ds(left_spin, 1)], (nv, nv)).T
    return left + virt_ref[pl.ds(right_spin, 1)]


def pair_energies(occ_ref, left_spin, right_spin, own):
    left = occ_ref[pl.ds(left_spin, 1)]
    chosen = lax.broadcasted_iota(jnp.int32, left.shape, 1) == own
    return jnp.sum(jnp.where(chosen, left, 0.0), axis=1, keepdims=True) + occ_ref[pl.ds(right_spin, 1)]


def amplitudes(coupling, occupied_pair, virtual_pair):
    return (coupling / (occupied_pair - virtual_pair)).astype(jnp.bfloat16)


def early_fit_kernel(orb_count, given_ref, *refs):
    *slices, factor_ref, early_ref, rows = refs
    factor_ref[...] = order_factor(given_ref, rows, orb_count)
    nv = early_ref.shape[1] // orb_count
    depth = early_depth(slices)
    for start in range(0, orb_count, GROUP):
        raw = [jnp.concatenate(list(pieces(slices, j)), axis=0) for j in range(start, start + GROUP)]
        columns = slice(start * nv, (start + GROUP) * nv)
        early_ref[:, columns] = dot(factor_ref[:, :depth], jnp.concatenate(raw, axis=1), NN)


def early_depth(slices):
    return sum(s.shape[-2] * (1 if len(s.shape) == 3 else s.shape[0]) for s in slices)


def fit_same_kernel(occ_ref, virt_ref, factor_ref, early_ref, *refs):
    slices, (fitted_ref, amp_ref, dens_ref, left, sums) = refs[:-5], refs[-5:]
    first = factor_ref.shape[0] - early_depth(slices)
    spin, own = lax.axis_index("spin"), lax.axis_index("orb")
    count, nv = occ_ref.shape[1], virt_ref.shape[1]
    sums[...] = energy_sums(virt_ref, spin, spin)
    energies = pair_energies(occ_ref, spin, spin, own)
    raw = jnp.concatenate(list(pieces(slices, own)), axis=0)
    early = early_ref[:, pl.ds(pl.multiple_of(own * nv, nv), nv)]
    left[...] = (early + dot(factor_ref[:, first:], raw, NN)).astype(left.dtype).T
    total = None
    for start in range(0, count, GROUP):
        members = range(start, start + GROUP)
        raw = [jnp.concatenate(list(pieces(slices, j)), axis=0) for j in members]
        columns = slice(start * nv, (start + GROUP) * nv)
        late = dot(factor_ref[:, first:], jnp.concatenate(raw, axis=1), NN)
        fitted = (early_ref[:, columns] + late).astype(fitted_ref.dtype)
        fitted_ref[:, columns] = fitted
        couplings = dot(left[...], fitted, NN)
        amps = []
        for n, j in enumerate(members):
            coupling = couplings[:, n * nv : (n + 1) * nv]
            amps.append(amplitudes(coupling - coupling.T, energies[:, j : j + 1], sums[...]))
        amps = jnp.concatenate(amps, axis=1)
        amp_ref[:, columns] = amps
        term = dot(amps, amps, NT)
        total = term if total is None else total + term
    dens_ref[...] = 0.5 * total


def opposite_all_kernel(
    occ_ref, virt_ref, factor_ref, early_ref, late_ref, last_ref, fitted_ref, dens_in,
    amp_ref, kept_ref, sent_ref, left, sums, dens,
):
    spin, own = lax.axis_index("spin"), lax.axis_index("orb")
    count, nv = occ_ref.shape[1], virt_ref.shape[1]
    sums[...] = energy_sums(virt_ref, 1 - spin, spin)
    energies = pair_energies(occ_ref, 1 - spin, spin, own)
    raw = jnp.concatenate([early_ref[...], late_ref[...], last_ref[...]], axis=0)
    left[...] = dot(factor_ref[...], raw, NN).astype(left.dtype).T
    total = dens_in[...]
    for start in range(0, count, GROUP):
        columns = slice(start * nv, (start + GROUP) * nv)
        couplings = dot(left[...], fitted_ref[:, columns], NN)
        amps = []
        for n in range(GROUP):
            energy = energies[:, start + n : start + n + 1]
            amps.append(amplitudes(couplings[:, n * nv : (n + 1) * nv], energy, sums[...]))
        amp_ref[:, columns] = jnp.concatenate(amps, axis=1)
        stacked = jnp.concatenate(amps, axis=0)
        total = total + dot(stacked, stacked, TN)
    dens[...] = total / count
    chip, core = own // 2, own % 2
    near, far, rows, _ = kept_ref.shape
    for ref, lane in ((kept_ref, core), (sent_ref, 1 - core)):
        for m in range(near):
            for n in range(far):
                there = ((chip ^ (near * lane + m)) & (2 * near - 1)) + 2 * near * n
                ref[m, n] = dens[pl.ds(pl.multiple_of(there * rows, rows), rows)]


def gamma_kernel(amp_ref, fitted_ref, *out_refs):
    rows = out_refs[0].shape[0]
    gamma = dot(amp_ref[...], fitted_ref[...], NT)
    for n, ref in enumerate(out_refs):
        ref[...] = gamma[n * rows : (n + 1) * rows].astype(ref.dtype)


def near_kernel(kept_in, arrived, *refs):
    one_ref, two_ref, total = refs[-3:]
    total[...] = kept_in[...] + arrived[...]
    core = lax.axis_index("orb") % 2
    one_ref[...] = total[1 - core]
    two_ref[...] = total[core]


def far_split_kernel(one_in, two_in, *refs):
    kept_ref, sent_ref, total = refs[-3:]
    total[...] = one_in[...] + two_in[...]
    mine = lax.axis_index("orb") // 8
    kept_ref[...] = total[mine]
    sent_ref[...] = total[1 - mine]


def core_split_kernel(kept_in, arrived, *refs):
    kept_ref, sent_ref, total = refs[-3:]
    total[...] = kept_in[...] + arrived[...]
    core, rows = lax.axis_index("orb") % 2, kept_ref.shape[0]
    kept_ref[...] = total[pl.ds(pl.multiple_of(core * rows, rows), rows)]
    sent_ref[...] = total[pl.ds(pl.multiple_of((1 - core) * rows, rows), rows)]


def finish_kernel(kept_in, arrived, gamma_in, *refs):
    *returned, gamma_ref, density_ref = refs
    rows = returned[0].shape[0]
    for n, ref in enumerate(returned):
        part = slice(n * rows, (n + 1) * rows)
        gamma_ref[part] = gamma_in[part] + ref[...].astype(jnp.float32)
    density_ref[0] = kept_in[...] + arrived[...]


def vmem_call(kernel, name, operands, outs, scratch=(), flops=0, in_hbm=0, pin=True):
    vmem, hbm = pl.BlockSpec(memory_space=pltpu.VMEM), pl.BlockSpec(memory_space=pltpu.HBM)
    moved = sum(a.size * a.dtype.itemsize for a in operands) if flops else 0
    if pin:
        places = [pltpu.HBM] * in_hbm + [pltpu.VMEM] * (len(operands) - in_hbm)
        operands = [pltpu.with_memory_space_constraint(*pair) for pair in zip(operands, places)]
    return pl.pallas_call(
        kernel,
        in_specs=[hbm] * in_hbm + [vmem] * (len(operands) - in_hbm),
        out_specs=[vmem] * len(outs),
        out_shape=[pltpu.VMEM(*out) if pin else jax.ShapeDtypeStruct(*out) for out in outs],
        scratch_shapes=[pltpu.VMEM(*s) if isinstance(s, tuple) else s for s in scratch],
        compiler_params=pltpu.CompilerParams(vmem_limit_bytes=VMEM_LIMIT),
        cost_estimate=pl.CostEstimate(flops=flops, bytes_accessed=moved, transcendentals=0),
        name=name,
    )(*operands)


def local_in_vmem(integrals, metric_factor, occ_energy, virt_energy, orb_count):
    across = [(0, 1), (1, 0)]
    swap = [(d, d ^ 1) for d in range(orb_count)]
    moves = ring_moves(orb_count)
    own = jnp.swapaxes(integrals[0], 1, 2)
    count, width, nv = own.shape
    naux = metric_factor.shape[0]
    half, full = jnp.bfloat16, jnp.float32
    depth = lambda part: width * sum(1 if s.ndim == 3 else s.shape[0] for s in part)

    pair = 2 * count * nv * nv
    steps = orb_count // 4
    lanes = [own, lax.ppermute(own, "orb", swap)]
    slices, swapped, early_row = lanes[1:], [], None
    for step in range(1, steps + 1):
        back = lanes[1:] if step == 1 else []
        lanes = [lax.ppermute(lane, "orb", moves) for lane in (lanes if step < steps else lanes[:1])]
        slices += lanes
        if step == steps - 2:
            sent = len(slices)
            (row,) = vmem_call(row_kernel, "early_row", slices, [((depth(slices), nv), half)])
            early_row = lax.ppermute(row, "spin", across)
        if step == steps - 1:
            factor, early = vmem_call(
                functools.partial(early_fit_kernel, orb_count), "early_fit", [metric_factor] + slices[: sent + 1],
                [((naux, naux), half), ((naux, count * nv), full)], [((naux, naux), half)], flops=0,
            )
        order = [early_row] if step == steps - 1 else [early] if step == steps else []
        (stacked,) = vmem_call(
            functools.partial(stack_kernel, len(lanes + back)), "stack", lanes + back + order,
            [((len(lanes + back),) + own.shape, half)],
        )
        swapped.append(lax.ppermute(stacked, "orb", swap))
        if step >= steps - 2:
            slices += swapped
            swapped = []
    rows_sent, cut = [early_row], sent+4
    for part in (slices[sent:cut], slices[cut:]):
        (row,) = vmem_call(row_kernel, "late_row", part, [((depth(part), nv), half)])
        rows_sent.append(lax.ppermute(row, "spin", across))
    fitted, amp_same, dens_same = vmem_call(
        fit_same_kernel, "fit_same", [occ_energy, virt_energy, factor, early] + slices[sent + 1 :],
        [((naux, count * nv), half), ((nv, count * nv), half), ((nv, nv), full)],
        [((nv, naux), half), ((nv, nv), full)],
    )
    rows = 2 * nv // orb_count
    share = (2, 2, rows, nv)
    amp_other, kept, sent = vmem_call(
        opposite_all_kernel, "opposite",
        [occ_energy, virt_energy, factor] + rows_sent + [fitted, dens_same],
        [((nv, count * nv), half)] + [(share, full)] * 2,
        [((nv, naux), half), ((nv, nv), full), ((nv, nv), full)],
        flops=pair * (naux + nv),
    )
    gamma_other = vmem_call(
        gamma_kernel, "gamma_other", [amp_other, fitted], [((nv // PIECES, naux), half)] * PIECES,
        flops=pair * naux,
    )
    (gamma_same,) = vmem_call(
        gamma_kernel, "gamma_same", [amp_same, fitted], [((nv, naux), full)], flops=2*pair*naux
    )
    returned = [lax.ppermute(piece, "spin", across) for piece in gamma_other]
    arrived = lax.ppermute(sent, "orb", swap)
    one, two = vmem_call(near_kernel, "near", [kept, arrived], [(share[1:], full)] * 2, [(share, full)])
    chip_moves = lambda first, second: [
        (d, 2 * (d // 2 ^ (second if d % 2 else first)) + d % 2) for d in range(orb_count)
    ]
    one = lax.ppermute(one, "orb", chip_moves(1, 2))
    two = lax.ppermute(two, "orb", chip_moves(0, 3))
    kept, sent = vmem_call(
        far_split_kernel, "far_split", [one, two], [(share[2:], full)] * 2, [(share[1:], full)]
    )
    arrived = lax.ppermute(sent, "orb", chip_moves(4, 4))
    kept, sent = vmem_call(
        core_split_kernel, "core_split", [kept, arrived, gamma_same], [((rows // 2, nv), full)] * 2, [(share[2:], full)]
    )
    arrived = lax.ppermute(sent, "orb", swap)
    gamma, density = vmem_call(
        finish_kernel, "finish", [kept, arrived, gamma_same] + returned,
        [((nv, naux), full), ((1, rows // 2, nv), full)], pin=False,
    )
    return gamma[None, None], density


def fit_kernel(factor_ref, *refs):
    slices, out_ref = refs[:-1], refs[-1]
    for g in range(out_ref.shape[0]):
        raw = jnp.concatenate([piece[g] for piece in slices], axis=0)
        out_ref[g] = dot(factor_ref[...], raw, NN).astype(out_ref.dtype)


def fit(factor, slices, group):
    count, _, virt = slices[0].shape
    naux = factor.shape[0]
    return pl.pallas_call(
        fit_kernel,
        grid=(count // group,),
        in_specs=[pl.BlockSpec(factor.shape, lambda j: (0, 0))]
        + [pl.BlockSpec((group,) + s.shape[1:], lambda j: (j, 0, 0)) for s in slices],
        out_specs=pl.BlockSpec((group, naux, virt), lambda j: (j, 0, 0)),
        out_shape=jax.ShapeDtypeStruct((count, naux, virt), jnp.bfloat16),
        compiler_params=pltpu.CompilerParams(vmem_limit_bytes=VMEM_LIMIT),
        name="fit",
    )(factor, *slices)


def same_kernel(own_ref, pair_ref, own_block, blocks, v_col, v_row, gamma_ref, dens_ref, left):
    step = pl.program_id(0)

    @pl.when(step == 0)
    def _():
        left[...] = own_block[0].T
        gamma_ref[...] = jnp.zeros_like(gamma_ref)
        dens_ref[...] = jnp.zeros_like(dens_ref)

    group = blocks.shape[0]
    for g in range(group):
        right = blocks[g]
        coupling = dot(left[...], right, NN)
        coupling = coupling - coupling.T
        denominator = (pair_ref[step * group + g] - v_col[...]) - v_row[...]
        amplitude = (coupling / denominator).astype(jnp.bfloat16)
        gamma_ref[...] += dot(amplitude, right, NT)
        dens_ref[...] += 0.5 * dot(amplitude, amplitude, NT)


def same_spin(fitted, own_index, pair_energy, virt, group):
    count, naux, nv = fitted.shape
    whole = lambda shape: pl.BlockSpec(shape, lambda j, *_: (0,) * len(shape))
    return pl.pallas_call(
        same_kernel,
        grid_spec=pltpu.PrefetchScalarGridSpec(
            num_scalar_prefetch=2,
            grid=(count // group,),
            in_specs=[
                pl.BlockSpec((1, naux, nv), lambda j, own, pair: (own[0], 0, 0)),
                pl.BlockSpec((group, naux, nv), lambda j, own, pair: (j, 0, 0)),
                whole((nv, 1)),
                whole((1, nv)),
            ],
            out_specs=[whole((nv, naux)), whole((nv, nv))],
            scratch_shapes=[pltpu.VMEM((nv, naux), jnp.bfloat16)],
        ),
        out_shape=[
            jax.ShapeDtypeStruct((nv, naux), jnp.float32),
            jax.ShapeDtypeStruct((nv, nv), jnp.float32),
        ],
        compiler_params=pltpu.CompilerParams(vmem_limit_bytes=VMEM_LIMIT),
        name="same_spin",
    )(own_index, pair_energy, fitted, fitted, virt[:, None], virt[None, :])


def opposite_kernel(pair_ref, factor, raw, blocks, v_col, v_row, dens_in, gamma_ref, dens_ref, left):
    step = pl.program_id(0)

    @pl.when(step == 0)
    def _():
        left[...] = dot(factor[...], raw[...], NN).astype(left.dtype).T
        gamma_ref[...] = jnp.zeros_like(gamma_ref)
        dens_ref[...] = dens_in[...]

    group = blocks.shape[0]
    for g in range(group):
        right = blocks[g]
        coupling = dot(left[...], right, NN)
        denominator = (pair_ref[step * group + g] - v_col[...]) - v_row[...]
        amplitude = (coupling / denominator).astype(jnp.bfloat16)
        gamma_ref[...] += dot(amplitude, right, NT)
        dens_ref[...] += dot(amplitude, amplitude, TN)


def opposite_spin(fitted, factor, raw, pair_energy, virt_left, virt_right, dens, group):
    count, naux, nv = fitted.shape
    whole = lambda shape: pl.BlockSpec(shape, lambda j, *_: (0,) * len(shape))
    return pl.pallas_call(
        opposite_kernel,
        grid_spec=pltpu.PrefetchScalarGridSpec(
            num_scalar_prefetch=1,
            grid=(count // group,),
            in_specs=[
                whole(factor.shape),
                whole(raw.shape),
                pl.BlockSpec((group, naux, nv), lambda j, pair: (j, 0, 0)),
                whole((nv, 1)),
                whole((1, nv)),
                whole((nv, nv)),
            ],
            out_specs=[whole((nv, naux)), whole((nv, nv))],
            scratch_shapes=[pltpu.VMEM((nv, naux), jnp.bfloat16)],
        ),
        out_shape=[
            jax.ShapeDtypeStruct((nv, naux), jnp.float32),
            jax.ShapeDtypeStruct((nv, nv), jnp.float32),
        ],
        compiler_params=pltpu.CompilerParams(vmem_limit_bytes=VMEM_LIMIT),
        name="opposite_spin",
    )(pair_energy, factor, raw, fitted, virt_left[:, None], virt_right[None, :], dens)


def reduce_rows(total, orb_count, keep):
    index = lax.axis_index("orb")
    bits = orb_count.bit_length() - 1
    rows = total.reshape((2,) * (bits - 1) + total.shape[1:])
    for bit in range(1, bits + 1 - keep.bit_length()):
        axis = bits - 1 - bit
        mine = (index >> bit) & 1
        moves = [(d, d ^ (1 << bit)) for d in range(orb_count)]
        kept = lax.dynamic_index_in_dim(rows, mine, axis, keepdims=False)
        sent = lax.dynamic_index_in_dim(rows, 1 - mine, axis, keepdims=False)
        arrived = lax.ppermute(sent, "orb", moves)
        rows = kept + arrived
    return kept, arrived


def local_streamed(integrals, metric_factor, occ_energy, virt_energy, orb_count):
    spin_index = lax.axis_index("spin")
    orbit_index = lax.axis_index("orb")
    other_spin = 1 - spin_index
    pick = lambda array, n: lax.dynamic_index_in_dim(array, n, 0, keepdims=False)
    occ_same, occ_other = pick(occ_energy, spin_index), pick(occ_energy, other_spin)
    virt_same, virt_other = pick(virt_energy, spin_index), pick(virt_energy, other_spin)
    across = [(0, 1), (1, 0)]

    own = jnp.swapaxes(integrals[0], 1, 2)
    occupied, width, nv = own.shape
    naux = metric_factor.shape[0]
    sources = pick(jnp.asarray(slice_sources(orb_count)), orbit_index)
    factor = jnp.take(metric_factor.reshape(orb_count, width, naux), sources, axis=0)
    factor = factor.reshape(naux, naux).T

    slices = []
    for part in gather_slices(own, orb_count):
        slices += [part] if part.ndim == 3 else [part[n] for n in range(part.shape[0])]
    own_row = [pick(s, orbit_index) for s in slices]
    early = len(slices) - 6 if len(slices) > 8 else len(slices) // 2
    raw_row = jnp.concatenate(
        [
            lax.ppermute(jnp.concatenate(own_row[:early]), "spin", across),
            lax.ppermute(jnp.concatenate(own_row[early:]), "spin", across),
        ]
    )
    if width % 16:
        slices = [jnp.concatenate(slices, axis=1)]
    fitted = fit(factor, slices, 2)

    own_energy, other_energy = pick(occ_same, orbit_index), pick(occ_other, orbit_index)
    gamma_same, dens = same_spin(fitted, orbit_index[None], own_energy + occ_same, virt_same, 2)
    gamma_other, dens = opposite_spin(
        fitted, factor, raw_row, other_energy + occ_same, virt_other, virt_same, dens, 2
    )
    returned = lax.ppermute(gamma_other, "spin", across)
    gamma = gamma_same + returned
    split = dens.reshape(orb_count // 2, 2, nv // orb_count, nv) / occupied
    kept, sent = (lax.dynamic_index_in_dim(split, n, 1, False) for n in (orbit_index % 2, 1 - orbit_index % 2))
    swap = [(d, d ^ 1) for d in range(orb_count)]
    kept, arrived = reduce_rows(kept + lax.ppermute(sent, "orb", swap), orb_count, 1)
    density = kept + arrived
    return gamma[None, None], density[None]


def local(integrals, metric_factor, occ_energy, virt_energy, orb_count):
    _, count, nv, width = integrals.shape
    fits = orb_count == 16 and count * nv * metric_factor.shape[0] * 2 <= 4 * 1024 * 1024 and width % 16 == 0 and count % GROUP == 0
    chosen = local_in_vmem if fits else local_streamed
    return chosen(integrals, metric_factor, occ_energy, virt_energy, orb_count)


def solution(mesh):
    return jax.shard_map(
        functools.partial(local, orb_count=mesh.shape["orb"]),
        mesh=mesh,
        in_specs=(P("spin", None, None, "orb"), P(), P(), P()),
        out_specs=(P("spin", "orb", None, None), P("spin", "orb", None)),
        check_vma=False,
    )
```

```python
import functools

import jax
import jax.numpy as jnp
import numpy as np
from jax import lax
from jax.experimental import pallas as pl
from jax.experimental.pallas import tpu as pltpu
from jax.sharding import PartitionSpec as P

VMEM_LIMIT = 20 * 1024 * 1024
GROUP = 4
PIECES = 1
NN = (((1,), (0,)), ((), ()))
NT = (((1,), (1,)), ((), ()))
TN = (((0,), (0,)), ((), ()))


def dot(left, right, dims):
    return lax.dot_general(left, right, dims, preferred_element_type=jnp.float32)


def chip_ring(orb_count):
    chips = orb_count // 2
    order = list(range(0, chips, 2)) + list(range(chips - 1 - chips % 2, 0, -2))
    following = {order[r]: order[(r + 1) % chips] for r in range(chips)}
    return order, following


def ring_moves(orb_count):
    _, following = chip_ring(orb_count)
    forward = [(2 * p, 2 * q) for p, q in following.items()]
    backward = [(2 * q + 1, 2 * p + 1) for p, q in following.items()]
    return forward + backward


def slice_sources(orb_count):
    order, _ = chip_ring(orb_count)
    chips = len(order)
    place = {chip: r for r, chip in enumerate(order)}
    table = []
    for device in range(orb_count):
        chip, core = device // 2, device % 2
        sources = [device, device ^ 1]
        for step in range(1, chips // 2 + 1):
            ahead = order[(place[chip] + (step if core else -step)) % chips]
            behind = order[(place[chip] - (step if core else -step)) % chips]
            if 2 * step == chips:
                sources += [2 * ahead + core, 2 * behind + 1 - core]
            else:
                sources += [2 * ahead + core, 2 * ahead + 1 - core]
                sources += [2 * behind + 1 - core, 2 * behind + core]
        table.append(sources)
    return np.asarray(table, np.int32)


def gather_slices(own, orb_count):
    moves = ring_moves(orb_count)
    swap = [(d, d ^ 1) for d in range(orb_count)]
    chips = orb_count // 2
    lanes = [own, lax.ppermute(own, "orb", swap)]
    gathered = list(lanes)
    for step in range(1, chips // 2 + 1):
        if 2 * step == chips:
            lanes = lanes[:1]
        lanes = [lax.ppermute(lane, "orb", moves) for lane in lanes]
        swapped = lax.ppermute(jnp.stack(lanes), "orb", swap)
        gathered += lanes + [swapped]
    return gathered


def pieces(refs, orbital):
    for ref in refs:
        if len(ref.shape) == 3:
            yield ref[orbital]
        else:
            for lane in range(ref.shape[0]):
                yield ref[lane, orbital]


def order_factor(factor_ref, rows, orb_count):
    own = lax.axis_index("orb")
    chips, width = orb_count // 2, factor_ref.shape[0] // orb_count
    chip, core = own // 2, own % 2
    place = jnp.where(chip % 2 == 0, chip // 2, chips - (chip + 1) // 2)

    def chip_at(distance):
        there = (place + chips + jnp.where(core == 0, -distance, distance)) % chips
        return jnp.where(2 * there < chips, 2 * there, 2 * (chips - there) - 1)

    sources, first = [own ^ 1], []
    for step in range(1, chips // 2 + 1):
        ahead, behind = 2 * chip_at(step), 2 * chip_at(-step)
        back = [own] if step == 1 else []
        if 2 * step == chips:
            sources += [ahead + core, behind + 1 - core]
        elif step < chips // 2 - 1:
            sources += [ahead + core, ahead + 1 - core]
            first += [behind + 1 - core, behind + core] + back
        else:
            sources += first + [ahead + core, ahead + 1 - core, behind + 1 - core, behind + core] + back
            first = []
    for n, source in enumerate(sources):
        rows[n * width : (n + 1) * width] = factor_ref[pl.ds(pl.multiple_of(source * width, width), width)]
    return rows[...].T


def row_kernel(*refs):
    *slices, out_ref = refs
    out_ref[...] = jnp.concatenate(list(pieces(slices, lax.axis_index("orb"))), axis=0)


def stack_kernel(lanes, *refs):
    for n in range(lanes):
        refs[-1][n] = refs[n][...]


def energy_sums(virt_ref, left_spin, right_spin):
    nv = virt_ref.shape[1]
    left = jnp.broadcast_to(virt_ref[pl.ds(left_spin, 1)], (nv, nv)).T
    return left + virt_ref[pl.ds(right_spin, 1)]


def pair_energies(occ_ref, left_spin, right_spin, own):
    left = occ_ref[pl.ds(left_spin, 1)]
    chosen = lax.broadcasted_iota(jnp.int32, left.shape, 1) == own
    return jnp.sum(jnp.where(chosen, left, 0.0), axis=1, keepdims=True) + occ_ref[pl.ds(right_spin, 1)]


def amplitudes(coupling, occupied_pair, virtual_pair):
    return (coupling / (occupied_pair - virtual_pair)).astype(jnp.bfloat16)


def early_fit_kernel(orb_count, given_ref, *refs):
    *slices, factor_ref, early_ref, rows = refs
    factor_ref[...] = order_factor(given_ref, rows, orb_count)
    nv = early_ref.shape[1] // orb_count
    depth = early_depth(slices)
    for start in range(0, orb_count, GROUP):
        raw = [jnp.concatenate(list(pieces(slices, j)), axis=0) for j in range(start, start + GROUP)]
        columns = slice(start * nv, (start + GROUP) * nv)
        early_ref[:, columns] = dot(factor_ref[:, :depth], jnp.concatenate(raw, axis=1), NN)


def early_depth(slices):
    return sum(s.shape[-2] * (1 if len(s.shape) == 3 else s.shape[0]) for s in slices)


def fit_same_kernel(occ_ref, virt_ref, factor_ref, early_ref, *refs):
    slices, (fitted_ref, amp_ref, dens_ref, left, sums) = refs[:-5], refs[-5:]
    first = factor_ref.shape[0] - early_depth(slices)
    spin, own = lax.axis_index("spin"), lax.axis_index("orb")
    count, nv = occ_ref.shape[1], virt_ref.shape[1]
    sums[...] = energy_sums(virt_ref, spin, spin)
    energies = pair_energies(occ_ref, spin, spin, own)
    raw = jnp.concatenate(list(pieces(slices, own)), axis=0)
    early = early_ref[:, pl.ds(pl.multiple_of(own * nv, nv), nv)]
    left[...] = (early + dot(factor_ref[:, first:], raw, NN)).astype(left.dtype).T
    for start in range(0, count, GROUP):
        raw = [jnp.concatenate(list(pieces(slices, j)), axis=0) for j in range(start, start + GROUP)]
        columns = slice(start * nv, (start + GROUP) * nv)
        late = dot(factor_ref[:, first:], jnp.concatenate(raw, axis=1), NN)
        fitted_ref[:, columns] = (early_ref[:, columns] + late).astype(fitted_ref.dtype)
    total = None
    for start in range(0, count, GROUP):
        columns = slice(start * nv, (start + GROUP) * nv)
        couplings = dot(left[...], fitted_ref[:, columns], NN)
        amps = []
        for n in range(GROUP):
            coupling = couplings[:, n * nv : (n + 1) * nv]
            j = start + n
            amps.append(amplitudes(coupling - coupling.T, energies[:, j : j + 1], sums[...]))
        amps = jnp.concatenate(amps, axis=1)
        amp_ref[:, columns] = amps
        term = dot(amps, amps, NT)
        total = term if total is None else total + term
    dens_ref[...] = 0.5 * total


def opposite_all_kernel(
    occ_ref, virt_ref, factor_ref, early_ref, late_ref, last_ref, fitted_ref, dens_in,
    amp_ref, kept_ref, sent_ref, left, sums, dens,
):
    spin, own = lax.axis_index("spin"), lax.axis_index("orb")
    count, nv = occ_ref.shape[1], virt_ref.shape[1]
    sums[...] = energy_sums(virt_ref, 1 - spin, spin)
    energies = pair_energies(occ_ref, 1 - spin, spin, own)
    raw = jnp.concatenate([early_ref[...], late_ref[...], last_ref[...]], axis=0)
    left[...] = dot(factor_ref[...], raw, NN).astype(left.dtype).T
    total = dens_in[...]
    for start in range(0, count, GROUP):
        columns = slice(start * nv, (start + GROUP) * nv)
        couplings = dot(left[...], fitted_ref[:, columns], NN)
        amps = []
        for n in range(GROUP):
            energy = energies[:, start + n : start + n + 1]
            amps.append(amplitudes(couplings[:, n * nv : (n + 1) * nv], energy, sums[...]))
        amp_ref[:, columns] = jnp.concatenate(amps, axis=1)
        stacked = jnp.concatenate(amps, axis=0)
        total = total + dot(stacked, stacked, TN)
    dens[...] = total / count
    chip, core = own // 2, own % 2
    near, far, rows, _ = kept_ref.shape
    for ref, lane in ((kept_ref, core), (sent_ref, 1 - core)):
        for m in range(near):
            for n in range(far):
                offset = lane + m * (3 - 2 * lane)
                there = ((chip ^ offset) & (2 * near - 1)) + 2 * near * n
                ref[m, n] = dens[pl.ds(pl.multiple_of(there * rows, rows), rows)]


def gamma_kernel(amp_ref, fitted_ref, *out_refs):
    rows = out_refs[0].shape[0]
    gamma = dot(amp_ref[...], fitted_ref[...], NT)
    for n, ref in enumerate(out_refs):
        ref[...] = gamma[n * rows : (n + 1) * rows].astype(ref.dtype)


def near_kernel(kept_in, arrived, *refs):
    one_ref, two_ref, total = refs[-3:]
    total[...] = kept_in[...] + arrived[...]
    core = lax.axis_index("orb") % 2
    one_ref[...] = total[1 - core]
    two_ref[...] = total[core]


def far_split_kernel(one_in, two_in, *refs):
    kept_ref, sent_ref, total = refs[-3:]
    total[...] = one_in[...] + two_in[...]
    mine = lax.axis_index("orb") // (lax.axis_size("orb") // 2)
    kept_ref[...] = total[mine]
    sent_ref[...] = total[1 - mine]


def core_split_kernel(kept_in, arrived, *refs):
    kept_ref, sent_ref, total = refs[-3:]
    total[...] = kept_in[...] + arrived[...]
    core, rows = lax.axis_index("orb") % 2, kept_ref.shape[0]
    kept_ref[...] = total[pl.ds(pl.multiple_of(core * rows, rows), rows)]
    sent_ref[...] = total[pl.ds(pl.multiple_of((1 - core) * rows, rows), rows)]


def finish_kernel(kept_in, arrived, gamma_in, *refs):
    *returned, gamma_ref, density_ref = refs
    rows = returned[0].shape[0]
    for n, ref in enumerate(returned):
        part = slice(n * rows, (n + 1) * rows)
        gamma_ref[part] = gamma_in[part] + ref[...].astype(jnp.float32)
    density_ref[0] = kept_in[...] + arrived[...]


def vmem_call(kernel, name, operands, outs, scratch=(), flops=0, in_hbm=0, pin=True):
    vmem, hbm = pl.BlockSpec(memory_space=pltpu.VMEM), pl.BlockSpec(memory_space=pltpu.HBM)
    moved = sum(a.size * a.dtype.itemsize for a in operands) if flops else 0
    if pin:
        places = [pltpu.HBM] * in_hbm + [pltpu.VMEM] * (len(operands) - in_hbm)
        operands = [pltpu.with_memory_space_constraint(*pair) for pair in zip(operands, places)]
    return pl.pallas_call(
        kernel,
        in_specs=[hbm] * in_hbm + [vmem] * (len(operands) - in_hbm),
        out_specs=[vmem] * len(outs),
        out_shape=[pltpu.VMEM(*out) if pin else jax.ShapeDtypeStruct(*out) for out in outs],
        scratch_shapes=[pltpu.VMEM(*s) if isinstance(s, tuple) else s for s in scratch],
        compiler_params=pltpu.CompilerParams(vmem_limit_bytes=VMEM_LIMIT),
        cost_estimate=pl.CostEstimate(flops=flops, bytes_accessed=moved, transcendentals=0),
        name=name,
    )(*operands)


def local_in_vmem(integrals, metric_factor, occ_energy, virt_energy, orb_count):
    across = [(0, 1), (1, 0)]
    swap = [(d, d ^ 1) for d in range(orb_count)]
    moves = ring_moves(orb_count)
    own = jnp.swapaxes(integrals[0], 1, 2)
    count, width, nv = own.shape
    naux = metric_factor.shape[0]
    half, full = jnp.bfloat16, jnp.float32
    depth = lambda part: width * sum(1 if s.ndim == 3 else s.shape[0] for s in part)

    pair = 2 * count * nv * nv
    steps = orb_count // 4
    lanes = [own, lax.ppermute(own, "orb", swap)]
    slices, swapped, early_row = lanes[1:], [], None
    for step in range(1, steps + 1):
        back = lanes[1:] if step == 1 else []
        lanes = [lax.ppermute(lane, "orb", moves) for lane in (lanes if step < steps else lanes[:1])]
        slices += lanes
        if step == steps - 2:
            sent = len(slices)
            (row,) = vmem_call(row_kernel, "early_row", slices, [((depth(slices), nv), half)])
            early_row = lax.ppermute(row, "spin", across)
        if step == steps - 1:
            factor, early = vmem_call(
                functools.partial(early_fit_kernel, orb_count), "early_fit", [metric_factor] + slices[: sent + 1],
                [((naux, naux), half), ((naux, count * nv), full)], [((naux, naux), half)], flops=0,
            )
        order = [early_row] if step == steps - 1 else [early] if step == steps else []
        (stacked,) = vmem_call(
            functools.partial(stack_kernel, len(lanes + back)), "stack", lanes + back + order,
            [((len(lanes + back),) + own.shape, half)],
        )
        swapped.append(lax.ppermute(stacked, "orb", swap))
        if step >= steps - 2:
            slices += swapped
            swapped = []
    rows_sent, cut = [early_row], sent + 4
    for part in (slices[sent:cut], slices[cut:]):
        (row,) = vmem_call(row_kernel, "late_row", part, [((depth(part), nv), half)])
        rows_sent.append(lax.ppermute(row, "spin", across))
    fitted, amp_same, dens_same = vmem_call(
        fit_same_kernel, "fit_same", [occ_energy, virt_energy, factor, early] + slices[sent + 1 :],
        [((naux, count * nv), half), ((nv, count * nv), half), ((nv, nv), full)],
        [((nv, naux), half), ((nv, nv), full)],
    )
    rows = 2 * nv // orb_count
    share = (2, 2, rows, nv)
    amp_other, kept, sent = vmem_call(
        opposite_all_kernel, "opposite",
        [occ_energy, virt_energy, factor] + rows_sent + [fitted, dens_same],
        [((nv, count * nv), half)] + [(share, full)] * 2,
        [((nv, naux), half), ((nv, nv), full), ((nv, nv), full)],
        flops=pair * (naux + nv),
    )
    gamma_other = vmem_call(
        gamma_kernel, "gamma_other", [amp_other, fitted], [((nv // PIECES, naux), half)] * PIECES,
        flops=pair * naux,
    )
    (gamma_same,) = vmem_call(
        gamma_kernel, "gamma_same", [amp_same, fitted], [((nv, naux), full)], flops=2 * pair * naux
    )
    returned = [lax.ppermute(piece, "spin", across) for piece in gamma_other]
    arrived = lax.ppermute(sent, "orb", swap)
    one, two = vmem_call(near_kernel, "near", [kept, arrived] + list(gamma_other), [(share[1:], full)] * 2, [(share, full)])
    chip_moves = lambda first, second: [
        (d, 2 * (d // 2 ^ (second if d % 2 else first)) + d % 2) for d in range(orb_count)
    ]
    one = lax.ppermute(one, "orb", chip_moves(3, 1))
    two = lax.ppermute(two, "orb", chip_moves(0, 2))
    kept, sent = vmem_call(
        far_split_kernel, "far_split", [one, two], [(share[2:], full)] * 2, [(share[1:], full)]
    )
    arrived = lax.ppermute(sent, "orb", chip_moves(orb_count // 4, orb_count // 4))
    kept, sent = vmem_call(
        core_split_kernel, "core_split", [kept, arrived, gamma_same], [((rows // 2, nv), full)] * 2, [(share[2:], full)]
    )
    arrived = lax.ppermute(sent, "orb", swap)
    gamma, density = vmem_call(
        finish_kernel, "finish", [kept, arrived, gamma_same] + returned,
        [((nv, naux), full), ((1, rows // 2, nv), full)], pin=False,
    )
    return gamma[None, None], density


def fit_kernel(factor_ref, *refs):
    slices, out_ref = refs[:-1], refs[-1]
    for g in range(out_ref.shape[0]):
        raw = jnp.concatenate([piece[g] for piece in slices], axis=0)
        out_ref[g] = dot(factor_ref[...], raw, NN).astype(out_ref.dtype)


def fit(factor, slices, group):
    count, _, virt = slices[0].shape
    naux = factor.shape[0]
    return pl.pallas_call(
        fit_kernel,
        grid=(count // group,),
        in_specs=[pl.BlockSpec(factor.shape, lambda j: (0, 0))]
        + [pl.BlockSpec((group,) + s.shape[1:], lambda j: (j, 0, 0)) for s in slices],
        out_specs=pl.BlockSpec((group, naux, virt), lambda j: (j, 0, 0)),
        out_shape=jax.ShapeDtypeStruct((count, naux, virt), jnp.bfloat16),
        compiler_params=pltpu.CompilerParams(vmem_limit_bytes=VMEM_LIMIT),
        name="fit",
    )(factor, *slices)


def same_kernel(own_ref, pair_ref, own_block, blocks, v_col, v_row, gamma_ref, dens_ref, left):
    step = pl.program_id(0)

    @pl.when(step == 0)
    def _():
        left[...] = own_block[0].T
        gamma_ref[...] = jnp.zeros_like(gamma_ref)
        dens_ref[...] = jnp.zeros_like(dens_ref)

    group = blocks.shape[0]
    for g in range(group):
        right = blocks[g]
        coupling = dot(left[...], right, NN)
        coupling = coupling - coupling.T
        denominator = (pair_ref[step * group + g] - v_col[...]) - v_row[...]
        amplitude = (coupling / denominator).astype(jnp.bfloat16)
        gamma_ref[...] += dot(amplitude, right, NT)
        dens_ref[...] += 0.5 * dot(amplitude, amplitude, NT)


def same_spin(fitted, own_index, pair_energy, virt, group):
    count, naux, nv = fitted.shape
    whole = lambda shape: pl.BlockSpec(shape, lambda j, *_: (0,) * len(shape))
    return pl.pallas_call(
        same_kernel,
        grid_spec=pltpu.PrefetchScalarGridSpec(
            num_scalar_prefetch=2,
            grid=(count // group,),
            in_specs=[
                pl.BlockSpec((1, naux, nv), lambda j, own, pair: (own[0], 0, 0)),
                pl.BlockSpec((group, naux, nv), lambda j, own, pair: (j, 0, 0)),
                whole((nv, 1)),
                whole((1, nv)),
            ],
            out_specs=[whole((nv, naux)), whole((nv, nv))],
            scratch_shapes=[pltpu.VMEM((nv, naux), jnp.bfloat16)],
        ),
        out_shape=[
            jax.ShapeDtypeStruct((nv, naux), jnp.float32),
            jax.ShapeDtypeStruct((nv, nv), jnp.float32),
        ],
        compiler_params=pltpu.CompilerParams(vmem_limit_bytes=VMEM_LIMIT),
        name="same_spin",
    )(own_index, pair_energy, fitted, fitted, virt[:, None], virt[None, :])


def opposite_kernel(pair_ref, factor, raw, blocks, v_col, v_row, dens_in, gamma_ref, dens_ref, left):
    step = pl.program_id(0)

    @pl.when(step == 0)
    def _():
        left[...] = dot(factor[...], raw[...], NN).astype(left.dtype).T
        gamma_ref[...] = jnp.zeros_like(gamma_ref)
        dens_ref[...] = dens_in[...]

    group = blocks.shape[0]
    for g in range(group):
        right = blocks[g]
        coupling = dot(left[...], right, NN)
        denominator = (pair_ref[step * group + g] - v_col[...]) - v_row[...]
        amplitude = (coupling / denominator).astype(jnp.bfloat16)
        gamma_ref[...] += dot(amplitude, right, NT)
        dens_ref[...] += dot(amplitude, amplitude, TN)


def opposite_spin(fitted, factor, raw, pair_energy, virt_left, virt_right, dens, group):
    count, naux, nv = fitted.shape
    whole = lambda shape: pl.BlockSpec(shape, lambda j, *_: (0,) * len(shape))
    return pl.pallas_call(
        opposite_kernel,
        grid_spec=pltpu.PrefetchScalarGridSpec(
            num_scalar_prefetch=1,
            grid=(count // group,),
            in_specs=[
                whole(factor.shape),
                whole(raw.shape),
                pl.BlockSpec((group, naux, nv), lambda j, pair: (j, 0, 0)),
                whole((nv, 1)),
                whole((1, nv)),
                whole((nv, nv)),
            ],
            out_specs=[whole((nv, naux)), whole((nv, nv))],
            scratch_shapes=[pltpu.VMEM((nv, naux), jnp.bfloat16)],
        ),
        out_shape=[
            jax.ShapeDtypeStruct((nv, naux), jnp.float32),
            jax.ShapeDtypeStruct((nv, nv), jnp.float32),
        ],
        compiler_params=pltpu.CompilerParams(vmem_limit_bytes=VMEM_LIMIT),
        name="opposite_spin",
    )(pair_energy, factor, raw, fitted, virt_left[:, None], virt_right[None, :], dens)


def reduce_rows(total, orb_count, keep):
    index = lax.axis_index("orb")
    bits = orb_count.bit_length() - 1
    rows = total.reshape((2,) * (bits - 1) + total.shape[1:])
    for bit in range(1, bits + 1 - keep.bit_length()):
        axis = bits - 1 - bit
        mine = (index >> bit) & 1
        moves = [(d, d ^ (1 << bit)) for d in range(orb_count)]
        kept = lax.dynamic_index_in_dim(rows, mine, axis, keepdims=False)
        sent = lax.dynamic_index_in_dim(rows, 1 - mine, axis, keepdims=False)
        arrived = lax.ppermute(sent, "orb", moves)
        rows = kept + arrived
    return kept, arrived


def local_streamed(integrals, metric_factor, occ_energy, virt_energy, orb_count):
    spin_index = lax.axis_index("spin")
    orbit_index = lax.axis_index("orb")
    other_spin = 1 - spin_index
    pick = lambda array, n: lax.dynamic_index_in_dim(array, n, 0, keepdims=False)
    occ_same, occ_other = pick(occ_energy, spin_index), pick(occ_energy, other_spin)
    virt_same, virt_other = pick(virt_energy, spin_index), pick(virt_energy, other_spin)
    across = [(0, 1), (1, 0)]

    own = jnp.swapaxes(integrals[0], 1, 2)
    occupied, width, nv = own.shape
    naux = metric_factor.shape[0]
    sources = pick(jnp.asarray(slice_sources(orb_count)), orbit_index)
    factor = jnp.take(metric_factor.reshape(orb_count, width, naux), sources, axis=0)
    factor = factor.reshape(naux, naux).T

    slices = []
    for part in gather_slices(own, orb_count):
        slices += [part] if part.ndim == 3 else [part[n] for n in range(part.shape[0])]
    own_row = [pick(s, orbit_index) for s in slices]
    early = len(slices) - 6 if len(slices) > 8 else len(slices) // 2
    raw_row = jnp.concatenate(
        [
            lax.ppermute(jnp.concatenate(own_row[:early]), "spin", across),
            lax.ppermute(jnp.concatenate(own_row[early:]), "spin", across),
        ]
    )
    if width % 16:
        slices = [jnp.concatenate(slices, axis=1)]
    fitted = fit(factor, slices, 2)

    own_energy, other_energy = pick(occ_same, orbit_index), pick(occ_other, orbit_index)
    gamma_same, dens = same_spin(fitted, orbit_index[None], own_energy + occ_same, virt_same, 2)
    gamma_other, dens = opposite_spin(
        fitted, factor, raw_row, other_energy + occ_same, virt_other, virt_same, dens, 2
    )
    returned = lax.ppermute(gamma_other, "spin", across)
    gamma = gamma_same + returned
    split = dens.reshape(orb_count // 2, 2, nv // orb_count, nv) / occupied
    kept, sent = (lax.dynamic_index_in_dim(split, n, 1, False) for n in (orbit_index % 2, 1 - orbit_index % 2))
    swap = [(d, d ^ 1) for d in range(orb_count)]
    kept, arrived = reduce_rows(kept + lax.ppermute(sent, "orb", swap), orb_count, 1)
    density = kept + arrived
    return gamma[None, None], density[None]


def local(integrals, metric_factor, occ_energy, virt_energy, orb_count):
    _, count, nv, width = integrals.shape
    fits = orb_count // 2 == 4 * 2 and count * nv * metric_factor.shape[0] * 2 <= 4 * 1024 * 1024 and width % 16 == 0 and count % GROUP == 0
    chosen = local_in_vmem if fits else local_streamed
    return chosen(integrals, metric_factor, occ_energy, virt_energy, orb_count)


def solution(mesh):
    return jax.shard_map(
        functools.partial(local, orb_count=mesh.shape["orb"]),
        mesh=mesh,
        in_specs=(P("spin", None, None, "orb"), P(), P(), P()),
        out_specs=(P("spin", "orb", None, None), P("spin", "orb", None)),
        check_vma=False,
    )
```

```python
import functools

import jax
import jax.numpy as jnp
import numpy as np
from jax import lax
from jax.experimental import pallas as pl
from jax.experimental.pallas import tpu as pltpu
from jax.sharding import PartitionSpec as P

VMEM_LIMIT = 20 * 1024 * 1024
GROUP = 4
PIECES = 2
NN = (((1,), (0,)), ((), ()))
NT = (((1,), (1,)), ((), ()))
TN = (((0,), (0,)), ((), ()))


def dot(left, right, dims):
    return lax.dot_general(left, right, dims, preferred_element_type=jnp.float32)


def chip_ring(orb_count):
    chips = orb_count // 2
    order = list(range(0, chips, 2)) + list(range(chips - 1 - chips % 2, 0, -2))
    following = {order[r]: order[(r + 1) % chips] for r in range(chips)}
    return order, following


def ring_moves(orb_count):
    _, following = chip_ring(orb_count)
    forward = [(2 * p, 2 * q) for p, q in following.items()]
    backward = [(2 * q + 1, 2 * p + 1) for p, q in following.items()]
    return forward + backward


def slice_sources(orb_count):
    order, _ = chip_ring(orb_count)
    chips = len(order)
    place = {chip: r for r, chip in enumerate(order)}
    table = []
    for device in range(orb_count):
        chip, core = device // 2, device % 2
        sources = [device, device ^ 1]
        for step in range(1, chips // 2 + 1):
            ahead = order[(place[chip] + (step if core else -step)) % chips]
            behind = order[(place[chip] - (step if core else -step)) % chips]
            if 2 * step == chips:
                sources += [2 * ahead + core, 2 * behind + 1 - core]
            else:
                sources += [2 * ahead + core, 2 * ahead + 1 - core]
                sources += [2 * behind + 1 - core, 2 * behind + core]
        table.append(sources)
    return np.asarray(table, np.int32)


def gather_slices(own, orb_count):
    moves = ring_moves(orb_count)
    swap = [(d, d ^ 1) for d in range(orb_count)]
    chips = orb_count // 2
    lanes = [own, lax.ppermute(own, "orb", swap)]
    gathered = list(lanes)
    for step in range(1, chips // 2 + 1):
        if 2 * step == chips:
            lanes = lanes[:1]
        lanes = [lax.ppermute(lane, "orb", moves) for lane in lanes]
        swapped = lax.ppermute(jnp.stack(lanes), "orb", swap)
        gathered += lanes + [swapped]
    return gathered


def pieces(refs, orbital):
    for ref in refs:
        if len(ref.shape) == 3:
            yield ref[orbital]
        else:
            for lane in range(ref.shape[0]):
                yield ref[lane, orbital]


def order_factor(factor_ref, rows, orb_count):
    own = lax.axis_index("orb")
    chips, width = orb_count // 2, factor_ref.shape[0] // orb_count
    chip, core = own // 2, own % 2
    place = jnp.where(chip % 2 == 0, chip // 2, chips - (chip + 1) // 2)

    def chip_at(distance):
        there = (place + chips + jnp.where(core == 0, -distance, distance)) % chips
        return jnp.where(2 * there < chips, 2 * there, 2 * (chips - there) - 1)

    sources, first = [own ^ 1], []
    for step in range(1, chips // 2 + 1):
        ahead, behind = 2 * chip_at(step), 2 * chip_at(-step)
        back = [own] if step == 1 else []
        if 2 * step == chips:
            sources += [ahead + core, behind + 1 - core]
        elif step < chips // 2 - 1:
            sources += [ahead + core, ahead + 1 - core]
            first += [behind + 1 - core, behind + core] + back
        else:
            sources += first + [ahead + core, ahead + 1 - core, behind + 1 - core, behind + core] + back
            first = []
    for n, source in enumerate(sources):
        rows[n * width : (n + 1) * width] = factor_ref[pl.ds(pl.multiple_of(source * width, width), width)]
    return rows[...].T


def row_kernel(*refs):
    *slices, out_ref = refs
    out_ref[...] = jnp.concatenate(list(pieces(slices, lax.axis_index("orb"))), axis=0)


def stack_kernel(lanes, *refs):
    for n in range(lanes):
        refs[-1][n] = refs[n][...]


def energy_sums(virt_ref, left_spin, right_spin):
    nv = virt_ref.shape[1]
    left = jnp.broadcast_to(virt_ref[pl.ds(left_spin, 1)], (nv, nv)).T
    return left + virt_ref[pl.ds(right_spin, 1)]


def pair_energies(occ_ref, left_spin, right_spin, own):
    left = occ_ref[pl.ds(left_spin, 1)]
    chosen = lax.broadcasted_iota(jnp.int32, left.shape, 1) == own
    return jnp.sum(jnp.where(chosen, left, 0.0), axis=1, keepdims=True) + occ_ref[pl.ds(right_spin, 1)]


def amplitudes(coupling, occupied_pair, virtual_pair):
    return (coupling / (occupied_pair - virtual_pair)).astype(jnp.bfloat16)


def early_fit_kernel(orb_count, given_ref, *refs):
    *slices, factor_ref, early_ref, rows = refs
    factor_ref[...] = order_factor(given_ref, rows, orb_count)
    nv = early_ref.shape[1] // orb_count
    depth = early_depth(slices)
    for start in range(0, orb_count, GROUP):
        raw = [jnp.concatenate(list(pieces(slices, j)), axis=0) for j in range(start, start + GROUP)]
        columns = slice(start * nv, (start + GROUP) * nv)
        early_ref[:, columns] = dot(factor_ref[:, :depth], jnp.concatenate(raw, axis=1), NN)


def early_depth(slices):
    return sum(s.shape[-2] * (1 if len(s.shape) == 3 else s.shape[0]) for s in slices)


def fit_same_kernel(occ_ref, virt_ref, factor_ref, early_ref, *refs):
    slices, (fitted_ref, amp_ref, dens_ref, left, sums) = refs[:-5], refs[-5:]
    first = factor_ref.shape[0] - early_depth(slices)
    spin, own = lax.axis_index("spin"), lax.axis_index("orb")
    count, nv = occ_ref.shape[1], virt_ref.shape[1]
    sums[...] = energy_sums(virt_ref, spin, spin)
    energies = pair_energies(occ_ref, spin, spin, own)
    raw = jnp.concatenate(list(pieces(slices, own)), axis=0)
    early = early_ref[:, pl.ds(pl.multiple_of(own * nv, nv), nv)]
    left[...] = (early + dot(factor_ref[:, first:], raw, NN)).astype(left.dtype).T
    for start in range(0, count, GROUP):
        raw = [jnp.concatenate(list(pieces(slices, j)), axis=0) for j in range(start, start + GROUP)]
        columns = slice(start * nv, (start + GROUP) * nv)
        late = dot(factor_ref[:, first:], jnp.concatenate(raw, axis=1), NN)
        fitted_ref[:, columns] = (early_ref[:, columns] + late).astype(fitted_ref.dtype)
    total = None
    for start in range(0, count, GROUP):
        columns = slice(start * nv, (start + GROUP) * nv)
        couplings = dot(left[...], fitted_ref[:, columns], NN)
        amps = []
        for n in range(GROUP):
            coupling = couplings[:, n * nv : (n + 1) * nv]
            j = start + n
            amps.append(amplitudes(coupling - coupling.T, energies[:, j : j + 1], sums[...]))
        amps = jnp.concatenate(amps, axis=1)
        amp_ref[:, columns] = amps
        term = dot(amps, amps, NT)
        total = term if total is None else total + term
    dens_ref[...] = 0.5 * total


def opposite_all_kernel(
    occ_ref, virt_ref, factor_ref, early_ref, late_ref, last_ref, fitted_ref, dens_in,
    amp_ref, kept_ref, sent_ref, left, sums, dens,
):
    spin, own = lax.axis_index("spin"), lax.axis_index("orb")
    count, nv = occ_ref.shape[1], virt_ref.shape[1]
    sums[...] = energy_sums(virt_ref, 1 - spin, spin)
    energies = pair_energies(occ_ref, 1 - spin, spin, own)
    raw = jnp.concatenate([early_ref[...], late_ref[...], last_ref[...]], axis=0)
    left[...] = dot(factor_ref[...], raw, NN).astype(left.dtype).T
    total = dens_in[...]
    for start in range(0, count, GROUP):
        columns = slice(start * nv, (start + GROUP) * nv)
        couplings = dot(left[...], fitted_ref[:, columns], NN)
        amps = []
        for n in range(GROUP):
            energy = energies[:, start + n : start + n + 1]
            amps.append(amplitudes(couplings[:, n * nv : (n + 1) * nv], energy, sums[...]))
        amp_ref[:, columns] = jnp.concatenate(amps, axis=1)
        stacked = jnp.concatenate(amps, axis=0)
        total = total + dot(stacked, stacked, TN)
    dens[...] = total / count
    chip, core = own // 2, own % 2
    near, far, rows, _ = kept_ref.shape
    for ref, lane in ((kept_ref, core), (sent_ref, 1 - core)):
        for m in range(near):
            for n in range(far):
                offset = lane + m * (3 - 2 * lane)
                there = ((chip ^ offset) & (2 * near - 1)) + 2 * near * n
                ref[m, n] = dens[pl.ds(pl.multiple_of(there * rows, rows), rows)]


def gamma_kernel(amp_ref, fitted_ref, *out_refs):
    rows = out_refs[0].shape[0]
    gamma = dot(amp_ref[...], fitted_ref[...], NT)
    for n, ref in enumerate(out_refs):
        ref[...] = gamma[n * rows : (n + 1) * rows].astype(ref.dtype)


def near_kernel(kept_in, arrived, *refs):
    one_ref, two_ref, total = refs[-3:]
    total[...] = kept_in[...] + arrived[...]
    core = lax.axis_index("orb") % 2
    one_ref[...] = total[1 - core]
    two_ref[...] = total[core]


def far_split_kernel(one_in, two_in, *refs):
    kept_ref, sent_ref, total = refs[-3:]
    total[...] = one_in[...] + two_in[...]
    mine = lax.axis_index("orb") // (lax.axis_size("orb") // 2)
    kept_ref[...] = total[mine]
    sent_ref[...] = total[1 - mine]


def core_split_kernel(kept_in, arrived, *refs):
    kept_ref, sent_ref, total = refs[-3:]
    total[...] = kept_in[...] + arrived[...]
    core, rows = lax.axis_index("orb") % 2, kept_ref.shape[0]
    kept_ref[...] = total[pl.ds(pl.multiple_of(core * rows, rows), rows)]
    sent_ref[...] = total[pl.ds(pl.multiple_of((1 - core) * rows, rows), rows)]


def finish_kernel(kept_in, arrived, gamma_in, *refs):
    *returned, gamma_ref, density_ref = refs
    rows = returned[0].shape[0]
    for n, ref in enumerate(returned):
        part = slice(n * rows, (n + 1) * rows)
        gamma_ref[part] = gamma_in[part] + ref[...].astype(jnp.float32)
    density_ref[0] = kept_in[...] + arrived[...]


def vmem_call(kernel, name, operands, outs, scratch=(), flops=0, in_hbm=0, pin=True):
    vmem, hbm = pl.BlockSpec(memory_space=pltpu.VMEM), pl.BlockSpec(memory_space=pltpu.HBM)
    moved = sum(a.size * a.dtype.itemsize for a in operands) if flops else 0
    if pin:
        places = [pltpu.HBM] * in_hbm + [pltpu.VMEM] * (len(operands) - in_hbm)
        operands = [pltpu.with_memory_space_constraint(*pair) for pair in zip(operands, places)]
    return pl.pallas_call(
        kernel,
        in_specs=[hbm] * in_hbm + [vmem] * (len(operands) - in_hbm),
        out_specs=[vmem] * len(outs),
        out_shape=[pltpu.VMEM(*out) if pin else jax.ShapeDtypeStruct(*out) for out in outs],
        scratch_shapes=[pltpu.VMEM(*s) if isinstance(s, tuple) else s for s in scratch],
        compiler_params=pltpu.CompilerParams(vmem_limit_bytes=VMEM_LIMIT),
        cost_estimate=pl.CostEstimate(flops=flops, bytes_accessed=moved, transcendentals=0),
        name=name,
    )(*operands)


def local_in_vmem(integrals, metric_factor, occ_energy, virt_energy, orb_count):
    across = [(0, 1), (1, 0)]
    swap = [(d, d ^ 1) for d in range(orb_count)]
    moves = ring_moves(orb_count)
    own = jnp.swapaxes(integrals[0], 1, 2)
    count, width, nv = own.shape
    naux = metric_factor.shape[0]
    half, full = jnp.bfloat16, jnp.float32
    depth = lambda part: width * sum(1 if s.ndim == 3 else s.shape[0] for s in part)

    pair = 2 * count * nv * nv
    steps = orb_count // 4
    lanes = [own, lax.ppermute(own, "orb", swap)]
    slices, swapped, early_row = lanes[1:], [], None
    for step in range(1, steps + 1):
        back = lanes[1:] if step == 1 else []
        lanes = [lax.ppermute(lane, "orb", moves) for lane in (lanes if step < steps else lanes[:1])]
        slices += lanes
        if step == steps - 2:
            sent = len(slices)
            (row,) = vmem_call(row_kernel, "early_row", slices, [((depth(slices), nv), half)])
            early_row = lax.ppermute(row, "spin", across)
        if step == steps - 1:
            factor, early = vmem_call(
                functools.partial(early_fit_kernel, orb_count), "early_fit", [metric_factor] + slices[: sent + 1],
                [((naux, naux), half), ((naux, count * nv), full)], [((naux, naux), half)], flops=0,
            )
        order = [early_row] if step == steps - 1 else [early] if step == steps else []
        (stacked,) = vmem_call(
            functools.partial(stack_kernel, len(lanes + back)), "stack", lanes + back + order,
            [((len(lanes + back),) + own.shape, half)],
        )
        swapped.append(lax.ppermute(stacked, "orb", swap))
        if step >= steps - 2:
            slices += swapped
            swapped = []
    rows_sent, cut = [early_row], sent + 3
    for part in (slices[sent:cut], slices[cut:]):
        (row,) = vmem_call(row_kernel, "late_row", part, [((depth(part), nv), half)])
        rows_sent.append(lax.ppermute(row, "spin", across))
    fitted, amp_same, dens_same = vmem_call(
        fit_same_kernel, "fit_same", [occ_energy, virt_energy, factor, early] + slices[sent + 1 :],
        [((naux, count * nv), half), ((nv, count * nv), half), ((nv, nv), full)],
        [((nv, naux), half), ((nv, nv), full)],
    )
    rows = 2 * nv // orb_count
    share = (2, 2, rows, nv)
    amp_other, kept, sent = vmem_call(
        opposite_all_kernel, "opposite",
        [occ_energy, virt_energy, factor] + rows_sent + [fitted, dens_same],
        [((nv, count * nv), half)] + [(share, full)] * 2,
        [((nv, naux), half), ((nv, nv), full), ((nv, nv), full)],
        flops=pair * (naux + nv),
    )
    gamma_other = vmem_call(
        gamma_kernel, "gamma_other", [amp_other, fitted], [((nv // PIECES, naux), half)] * PIECES,
        flops=pair * naux,
    )
    (gamma_same,) = vmem_call(
        gamma_kernel, "gamma_same", [amp_same, fitted], [((nv, naux), full)], flops=3 * pair * naux
    )
    returned = [lax.ppermute(piece, "spin", across) for piece in gamma_other]
    arrived = lax.ppermute(sent, "orb", swap)
    one, two = vmem_call(near_kernel, "near", [kept, arrived] + list(gamma_other), [(share[1:], full)] * 2, [(share, full)])
    chip_moves = lambda first, second: [
        (d, 2 * (d // 2 ^ (second if d % 2 else first)) + d % 2) for d in range(orb_count)
    ]
    one = lax.ppermute(one, "orb", chip_moves(3, 1))
    two = lax.ppermute(two, "orb", chip_moves(0, 2))
    kept, sent = vmem_call(
        far_split_kernel, "far_split", [one, two], [(share[2:], full)] * 2, [(share[1:], full)]
    )
    arrived = lax.ppermute(sent, "orb", chip_moves(orb_count // 4, orb_count // 4))
    kept, sent = vmem_call(
        core_split_kernel, "core_split", [kept, arrived, gamma_same], [((rows // 2, nv), full)] * 2, [(share[2:], full)]
    )
    arrived = lax.ppermute(sent, "orb", swap)
    gamma, density = vmem_call(
        finish_kernel, "finish", [kept, arrived, gamma_same] + returned,
        [((nv, naux), full), ((1, rows // 2, nv), full)], pin=False,
    )
    return gamma[None, None], density


def fit_kernel(factor_ref, *refs):
    slices, out_ref = refs[:-1], refs[-1]
    for g in range(out_ref.shape[0]):
        raw = jnp.concatenate([piece[g] for piece in slices], axis=0)
        out_ref[g] = dot(factor_ref[...], raw, NN).astype(out_ref.dtype)


def fit(factor, slices, group):
    count, _, virt = slices[0].shape
    naux = factor.shape[0]
    return pl.pallas_call(
        fit_kernel,
        grid=(count // group,),
        in_specs=[pl.BlockSpec(factor.shape, lambda j: (0, 0))]
        + [pl.BlockSpec((group,) + s.shape[1:], lambda j: (j, 0, 0)) for s in slices],
        out_specs=pl.BlockSpec((group, naux, virt), lambda j: (j, 0, 0)),
        out_shape=jax.ShapeDtypeStruct((count, naux, virt), jnp.bfloat16),
        compiler_params=pltpu.CompilerParams(vmem_limit_bytes=VMEM_LIMIT),
        name="fit",
    )(factor, *slices)


def same_kernel(own_ref, pair_ref, own_block, blocks, v_col, v_row, gamma_ref, dens_ref, left):
    step = pl.program_id(0)

    @pl.when(step == 0)
    def _():
        left[...] = own_block[0].T
        gamma_ref[...] = jnp.zeros_like(gamma_ref)
        dens_ref[...] = jnp.zeros_like(dens_ref)

    group = blocks.shape[0]
    for g in range(group):
        right = blocks[g]
        coupling = dot(left[...], right, NN)
        coupling = coupling - coupling.T
        denominator = (pair_ref[step * group + g] - v_col[...]) - v_row[...]
        amplitude = (coupling / denominator).astype(jnp.bfloat16)
        gamma_ref[...] += dot(amplitude, right, NT)
        dens_ref[...] += 0.5 * dot(amplitude, amplitude, NT)


def same_spin(fitted, own_index, pair_energy, virt, group):
    count, naux, nv = fitted.shape
    whole = lambda shape: pl.BlockSpec(shape, lambda j, *_: (0,) * len(shape))
    return pl.pallas_call(
        same_kernel,
        grid_spec=pltpu.PrefetchScalarGridSpec(
            num_scalar_prefetch=2,
            grid=(count // group,),
            in_specs=[
                pl.BlockSpec((1, naux, nv), lambda j, own, pair: (own[0], 0, 0)),
                pl.BlockSpec((group, naux, nv), lambda j, own, pair: (j, 0, 0)),
                whole((nv, 1)),
                whole((1, nv)),
            ],
            out_specs=[whole((nv, naux)), whole((nv, nv))],
            scratch_shapes=[pltpu.VMEM((nv, naux), jnp.bfloat16)],
        ),
        out_shape=[
            jax.ShapeDtypeStruct((nv, naux), jnp.float32),
            jax.ShapeDtypeStruct((nv, nv), jnp.float32),
        ],
        compiler_params=pltpu.CompilerParams(vmem_limit_bytes=VMEM_LIMIT),
        name="same_spin",
    )(own_index, pair_energy, fitted, fitted, virt[:, None], virt[None, :])


def opposite_kernel(pair_ref, factor, raw, blocks, v_col, v_row, dens_in, gamma_ref, dens_ref, left):
    step = pl.program_id(0)

    @pl.when(step == 0)
    def _():
        left[...] = dot(factor[...], raw[...], NN).astype(left.dtype).T
        gamma_ref[...] = jnp.zeros_like(gamma_ref)
        dens_ref[...] = dens_in[...]

    group = blocks.shape[0]
    for g in range(group):
        right = blocks[g]
        coupling = dot(left[...], right, NN)
        denominator = (pair_ref[step * group + g] - v_col[...]) - v_row[...]
        amplitude = (coupling / denominator).astype(jnp.bfloat16)
        gamma_ref[...] += dot(amplitude, right, NT)
        dens_ref[...] += dot(amplitude, amplitude, TN)


def opposite_spin(fitted, factor, raw, pair_energy, virt_left, virt_right, dens, group):
    count, naux, nv = fitted.shape
    whole = lambda shape: pl.BlockSpec(shape, lambda j, *_: (0,) * len(shape))
    return pl.pallas_call(
        opposite_kernel,
        grid_spec=pltpu.PrefetchScalarGridSpec(
            num_scalar_prefetch=1,
            grid=(count // group,),
            in_specs=[
                whole(factor.shape),
                whole(raw.shape),
                pl.BlockSpec((group, naux, nv), lambda j, pair: (j, 0, 0)),
                whole((nv, 1)),
                whole((1, nv)),
                whole((nv, nv)),
            ],
            out_specs=[whole((nv, naux)), whole((nv, nv))],
            scratch_shapes=[pltpu.VMEM((nv, naux), jnp.bfloat16)],
        ),
        out_shape=[
            jax.ShapeDtypeStruct((nv, naux), jnp.float32),
            jax.ShapeDtypeStruct((nv, nv), jnp.float32),
        ],
        compiler_params=pltpu.CompilerParams(vmem_limit_bytes=VMEM_LIMIT),
        name="opposite_spin",
    )(pair_energy, factor, raw, fitted, virt_left[:, None], virt_right[None, :], dens)


def reduce_rows(total, orb_count, keep):
    index = lax.axis_index("orb")
    bits = orb_count.bit_length() - 1
    rows = total.reshape((2,) * (bits - 1) + total.shape[1:])
    for bit in range(1, bits + 1 - keep.bit_length()):
        axis = bits - 1 - bit
        mine = (index >> bit) & 1
        moves = [(d, d ^ (1 << bit)) for d in range(orb_count)]
        kept = lax.dynamic_index_in_dim(rows, mine, axis, keepdims=False)
        sent = lax.dynamic_index_in_dim(rows, 1 - mine, axis, keepdims=False)
        arrived = lax.ppermute(sent, "orb", moves)
        rows = kept + arrived
    return kept, arrived


def local_streamed(integrals, metric_factor, occ_energy, virt_energy, orb_count):
    spin_index = lax.axis_index("spin")
    orbit_index = lax.axis_index("orb")
    other_spin = 1 - spin_index
    pick = lambda array, n: lax.dynamic_index_in_dim(array, n, 0, keepdims=False)
    occ_same, occ_other = pick(occ_energy, spin_index), pick(occ_energy, other_spin)
    virt_same, virt_other = pick(virt_energy, spin_index), pick(virt_energy, other_spin)
    across = [(0, 1), (1, 0)]

    own = jnp.swapaxes(integrals[0], 1, 2)
    occupied, width, nv = own.shape
    naux = metric_factor.shape[0]
    sources = pick(jnp.asarray(slice_sources(orb_count)), orbit_index)
    factor = jnp.take(metric_factor.reshape(orb_count, width, naux), sources, axis=0)
    factor = factor.reshape(naux, naux).T

    slices = []
    for part in gather_slices(own, orb_count):
        slices += [part] if part.ndim == 3 else [part[n] for n in range(part.shape[0])]
    own_row = [pick(s, orbit_index) for s in slices]
    early = len(slices) - 6 if len(slices) > 8 else len(slices) // 2
    raw_row = jnp.concatenate(
        [
            lax.ppermute(jnp.concatenate(own_row[:early]), "spin", across),
            lax.ppermute(jnp.concatenate(own_row[early:]), "spin", across),
        ]
    )
    if width % 16:
        slices = [jnp.concatenate(slices, axis=1)]
    fitted = fit(factor, slices, 2)

    own_energy, other_energy = pick(occ_same, orbit_index), pick(occ_other, orbit_index)
    gamma_same, dens = same_spin(fitted, orbit_index[None], own_energy + occ_same, virt_same, 2)
    gamma_other, dens = opposite_spin(
        fitted, factor, raw_row, other_energy + occ_same, virt_other, virt_same, dens, 2
    )
    returned = lax.ppermute(gamma_other, "spin", across)
    gamma = gamma_same + returned
    split = dens.reshape(orb_count // 2, 2, nv // orb_count, nv) / occupied
    kept, sent = (lax.dynamic_index_in_dim(split, n, 1, False) for n in (orbit_index % 2, 1 - orbit_index % 2))
    swap = [(d, d ^ 1) for d in range(orb_count)]
    kept, arrived = reduce_rows(kept + lax.ppermute(sent, "orb", swap), orb_count, 1)
    density = kept + arrived
    return gamma[None, None], density[None]


def local(integrals, metric_factor, occ_energy, virt_energy, orb_count):
    _, count, nv, width = integrals.shape
    fits = orb_count // 2 == 4 * 2 and count * nv * metric_factor.shape[0] * 2 <= 4 * 1024 * 1024 and width % 16 == 0 and count % GROUP == 0
    chosen = local_in_vmem if fits else local_streamed
    return chosen(integrals, metric_factor, occ_energy, virt_energy, orb_count)


def solution(mesh):
    return jax.shard_map(
        functools.partial(local, orb_count=mesh.shape["orb"]),
        mesh=mesh,
        in_specs=(P("spin", None, None, "orb"), P(), P(), P()),
        out_specs=(P("spin", "orb", None, None), P("spin", "orb", None)),
        check_vma=False,
    )
```

```python
import functools

import jax
import jax.numpy as jnp
import numpy as np
from jax import lax
from jax.experimental import pallas as pl
from jax.experimental.pallas import tpu as pltpu
from jax.sharding import PartitionSpec as P

VMEM_LIMIT = 20 * 1024 * 1024
GROUP = 4
PIECES = 1
NN = (((1,), (0,)), ((), ()))
NT = (((1,), (1,)), ((), ()))
TN = (((0,), (0,)), ((), ()))


def dot(left, right, dims):
    return lax.dot_general(left, right, dims, preferred_element_type=jnp.float32)


def chip_ring(orb_count):
    chips = orb_count // 2
    order = list(range(0, chips, 2)) + list(range(chips - 1 - chips % 2, 0, -2))
    following = {order[r]: order[(r + 1) % chips] for r in range(chips)}
    return order, following


def ring_moves(orb_count):
    _, following = chip_ring(orb_count)
    forward = [(2 * p, 2 * q) for p, q in following.items()]
    backward = [(2 * q + 1, 2 * p + 1) for p, q in following.items()]
    return forward + backward


def slice_sources(orb_count):
    order, _ = chip_ring(orb_count)
    chips = len(order)
    place = {chip: r for r, chip in enumerate(order)}
    table = []
    for device in range(orb_count):
        chip, core = device // 2, device % 2
        sources = [device, device ^ 1]
        for step in range(1, chips // 2 + 1):
            ahead = order[(place[chip] + (step if core else -step)) % chips]
            behind = order[(place[chip] - (step if core else -step)) % chips]
            if 2 * step == chips:
                sources += [2 * ahead + core, 2 * behind + 1 - core]
            else:
                sources += [2 * ahead + core, 2 * ahead + 1 - core]
                sources += [2 * behind + 1 - core, 2 * behind + core]
        table.append(sources)
    return np.asarray(table, np.int32)


def gather_slices(own, orb_count):
    moves = ring_moves(orb_count)
    swap = [(d, d ^ 1) for d in range(orb_count)]
    chips = orb_count // 2
    lanes = [own, lax.ppermute(own, "orb", swap)]
    gathered = list(lanes)
    for step in range(1, chips // 2 + 1):
        if 2 * step == chips:
            lanes = lanes[:1]
        lanes = [lax.ppermute(lane, "orb", moves) for lane in lanes]
        swapped = lax.ppermute(jnp.stack(lanes), "orb", swap)
        gathered += lanes + [swapped]
    return gathered


def pieces(refs, orbital):
    for ref in refs:
        if len(ref.shape) == 3:
            yield ref[orbital]
        else:
            for lane in range(ref.shape[0]):
                yield ref[lane, orbital]


def order_factor(factor_ref, rows, orb_count):
    own = lax.axis_index("orb")
    chips, width = orb_count // 2, factor_ref.shape[0] // orb_count
    chip, core = own // 2, own % 2
    place = jnp.where(chip % 2 == 0, chip // 2, chips - (chip + 1) // 2)

    def chip_at(distance):
        there = (place + chips + jnp.where(core == 0, -distance, distance)) % chips
        return jnp.where(2 * there < chips, 2 * there, 2 * (chips - there) - 1)

    sources, first = [own ^ 1], []
    for step in range(1, chips // 2 + 1):
        ahead, behind = 2 * chip_at(step), 2 * chip_at(-step)
        back = [own] if step == 1 else []
        if 2 * step == chips:
            sources += [ahead + core, behind + 1 - core]
        elif step < chips // 2 - 1:
            sources += [ahead + core, ahead + 1 - core]
            first += [behind + 1 - core, behind + core] + back
        else:
            sources += first + [ahead + core, ahead + 1 - core, behind + 1 - core, behind + core] + back
            first = []
    for n, source in enumerate(sources):
        rows[n * width : (n + 1) * width] = factor_ref[pl.ds(pl.multiple_of(source * width, width), width)]
    return rows[...].T


def row_kernel(*refs):
    *slices, out_ref = refs
    out_ref[...] = jnp.concatenate(list(pieces(slices, lax.axis_index("orb"))), axis=0)


def stack_kernel(lanes, *refs):
    for n in range(lanes):
        refs[-1][n] = refs[n][...]


def energy_sums(virt_ref, left_spin, right_spin):
    nv = virt_ref.shape[1]
    left = jnp.broadcast_to(virt_ref[pl.ds(left_spin, 1)], (nv, nv)).T
    return left + virt_ref[pl.ds(right_spin, 1)]


def pair_energies(occ_ref, left_spin, right_spin, own):
    left = occ_ref[pl.ds(left_spin, 1)]
    chosen = lax.broadcasted_iota(jnp.int32, left.shape, 1) == own
    return jnp.sum(jnp.where(chosen, left, 0.0), axis=1, keepdims=True) + occ_ref[pl.ds(right_spin, 1)]


def amplitudes(coupling, occupied_pair, virtual_pair):
    denominator = occupied_pair - virtual_pair
    inverse = pltpu.reciprocal(denominator, approx=True)
    inverse = inverse * (2.0 - denominator * inverse)
    return (coupling * inverse).astype(jnp.bfloat16)


def early_fit_kernel(orb_count, given_ref, *refs):
    *slices, factor_ref, early_ref, rows = refs
    factor_ref[...] = order_factor(given_ref, rows, orb_count)
    nv = early_ref.shape[1] // orb_count
    depth = early_depth(slices)
    for start in range(0, orb_count, GROUP):
        raw = [jnp.concatenate(list(pieces(slices, j)), axis=0) for j in range(start, start + GROUP)]
        columns = slice(start * nv, (start + GROUP) * nv)
        early_ref[:, columns] = dot(factor_ref[:, :depth], jnp.concatenate(raw, axis=1), NN)


def early_depth(slices):
    return sum(s.shape[-2] * (1 if len(s.shape) == 3 else s.shape[0]) for s in slices)


def fit_same_kernel(occ_ref, virt_ref, factor_ref, early_ref, *refs):
    slices, (fitted_ref, amp_ref, dens_ref, left, sums) = refs[:-5], refs[-5:]
    first = factor_ref.shape[0] - early_depth(slices)
    spin, own = lax.axis_index("spin"), lax.axis_index("orb")
    count, nv = occ_ref.shape[1], virt_ref.shape[1]
    sums[...] = energy_sums(virt_ref, spin, spin)
    energies = pair_energies(occ_ref, spin, spin, own)
    raw = jnp.concatenate(list(pieces(slices, own)), axis=0)
    early = early_ref[:, pl.ds(pl.multiple_of(own * nv, nv), nv)]
    left[...] = (early + dot(factor_ref[:, first:], raw, NN)).astype(left.dtype).T
    for start in range(0, count, GROUP):
        raw = [jnp.concatenate(list(pieces(slices, j)), axis=0) for j in range(start, start + GROUP)]
        columns = slice(start * nv, (start + GROUP) * nv)
        late = dot(factor_ref[:, first:], jnp.concatenate(raw, axis=1), NN)
        fitted_ref[:, columns] = (early_ref[:, columns] + late).astype(fitted_ref.dtype)
    total = None
    for start in range(0, count, GROUP):
        columns = slice(start * nv, (start + GROUP) * nv)
        couplings = dot(left[...], fitted_ref[:, columns], NN)
        amps = []
        for n in range(GROUP):
            coupling = couplings[:, n * nv : (n + 1) * nv]
            j = start + n
            amps.append(amplitudes(coupling - coupling.T, energies[:, j : j + 1], sums[...]))
        amps = jnp.concatenate(amps, axis=1)
        amp_ref[:, columns] = amps
        term = dot(amps, amps, NT)
        total = term if total is None else total + term
    dens_ref[...] = 0.5 * total


def opposite_all_kernel(
    occ_ref, virt_ref, factor_ref, early_ref, late_ref, last_ref, fitted_ref, dens_in,
    amp_ref, kept_ref, sent_ref, left, sums, dens,
):
    spin, own = lax.axis_index("spin"), lax.axis_index("orb")
    count, nv = occ_ref.shape[1], virt_ref.shape[1]
    sums[...] = energy_sums(virt_ref, 1 - spin, spin)
    energies = pair_energies(occ_ref, 1 - spin, spin, own)
    raw = jnp.concatenate([early_ref[...], late_ref[...], last_ref[...]], axis=0)
    left[...] = dot(factor_ref[...], raw, NN).astype(left.dtype).T
    total = dens_in[...]
    for start in range(0, count, GROUP):
        columns = slice(start * nv, (start + GROUP) * nv)
        couplings = dot(left[...], fitted_ref[:, columns], NN)
        amps = []
        for n in range(GROUP):
            energy = energies[:, start + n : start + n + 1]
            amps.append(amplitudes(couplings[:, n * nv : (n + 1) * nv], energy, sums[...]))
        amp_ref[:, columns] = jnp.concatenate(amps, axis=1)
        stacked = jnp.concatenate(amps, axis=0)
        total = total + dot(stacked, stacked, TN)
    dens[...] = total / count
    chip, core = own // 2, own % 2
    near, far, rows, _ = kept_ref.shape
    for ref, lane in ((kept_ref, core), (sent_ref, 1 - core)):
        for m in range(near):
            for n in range(far):
                offset = lane + m * (3 - 2 * lane)
                there = ((chip ^ offset) & (2 * near - 1)) + 2 * near * n
                ref[m, n] = dens[pl.ds(pl.multiple_of(there * rows, rows), rows)]


def gamma_kernel(amp_ref, fitted_ref, *out_refs):
    rows = out_refs[0].shape[0]
    gamma = dot(amp_ref[...], fitted_ref[...], NT)
    for n, ref in enumerate(out_refs):
        ref[...] = gamma[n * rows : (n + 1) * rows].astype(ref.dtype)


def near_kernel(kept_in, arrived, *refs):
    one_ref, two_ref, total = refs[-3:]
    total[...] = kept_in[...] + arrived[...]
    core = lax.axis_index("orb") % 2
    one_ref[...] = total[1 - core]
    two_ref[...] = total[core]


def far_split_kernel(one_in, two_in, *refs):
    kept_ref, sent_ref, total = refs[-3:]
    total[...] = one_in[...] + two_in[...]
    mine = lax.axis_index("orb") // (lax.axis_size("orb") // 2)
    kept_ref[...] = total[mine]
    sent_ref[...] = total[1 - mine]


def core_split_kernel(kept_in, arrived, *refs):
    kept_ref, sent_ref, total = refs[-3:]
    total[...] = kept_in[...] + arrived[...]
    core, rows = lax.axis_index("orb") % 2, kept_ref.shape[0]
    kept_ref[...] = total[pl.ds(pl.multiple_of(core * rows, rows), rows)]
    sent_ref[...] = total[pl.ds(pl.multiple_of((1 - core) * rows, rows), rows)]


def finish_kernel(kept_in, arrived, gamma_in, *refs):
    *returned, gamma_ref, density_ref = refs
    rows = returned[0].shape[0]
    for n, ref in enumerate(returned):
        part = slice(n * rows, (n + 1) * rows)
        gamma_ref[part] = gamma_in[part] + ref[...].astype(jnp.float32)
    density_ref[0] = kept_in[...] + arrived[...]


def vmem_call(kernel, name, operands, outs, scratch=(), flops=0, in_hbm=0, pin=True):
    vmem, hbm = pl.BlockSpec(memory_space=pltpu.VMEM), pl.BlockSpec(memory_space=pltpu.HBM)
    moved = sum(a.size * a.dtype.itemsize for a in operands) if flops else 0
    if pin:
        places = [pltpu.HBM] * in_hbm + [pltpu.VMEM] * (len(operands) - in_hbm)
        operands = [pltpu.with_memory_space_constraint(*pair) for pair in zip(operands, places)]
    return pl.pallas_call(
        kernel,
        in_specs=[hbm] * in_hbm + [vmem] * (len(operands) - in_hbm),
        out_specs=[vmem] * len(outs),
        out_shape=[pltpu.VMEM(*out) if pin else jax.ShapeDtypeStruct(*out) for out in outs],
        scratch_shapes=[pltpu.VMEM(*s) if isinstance(s, tuple) else s for s in scratch],
        compiler_params=pltpu.CompilerParams(vmem_limit_bytes=VMEM_LIMIT),
        cost_estimate=pl.CostEstimate(flops=flops, bytes_accessed=moved, transcendentals=0),
        name=name,
    )(*operands)


def local_in_vmem(integrals, metric_factor, occ_energy, virt_energy, orb_count):
    across = [(0, 1), (1, 0)]
    swap = [(d, d ^ 1) for d in range(orb_count)]
    moves = ring_moves(orb_count)
    own = jnp.swapaxes(integrals[0], 1, 2)
    count, width, nv = own.shape
    naux = metric_factor.shape[0]
    half, full = jnp.bfloat16, jnp.float32
    depth = lambda part: width * sum(1 if s.ndim == 3 else s.shape[0] for s in part)

    pair = 2 * count * nv * nv
    steps = orb_count // 4
    lanes = [own, lax.ppermute(own, "orb", swap)]
    slices, swapped, early_row = lanes[1:], [], None
    for step in range(1, steps + 1):
        back = lanes[1:] if step == 1 else []
        lanes = [lax.ppermute(lane, "orb", moves) for lane in (lanes if step < steps else lanes[:1])]
        slices += lanes
        if step == steps - 2:
            sent = len(slices)
            (row,) = vmem_call(row_kernel, "early_row", slices, [((depth(slices), nv), half)])
            early_row = lax.ppermute(row, "spin", across)
        if step == steps - 1:
            factor, early = vmem_call(
                functools.partial(early_fit_kernel, orb_count), "early_fit", [metric_factor] + slices[: sent + 1],
                [((naux, naux), half), ((naux, count * nv), full)], [((naux, naux), half)], flops=0,
            )
        order = [early_row] if step == steps - 1 else [early] if step == steps else []
        (stacked,) = vmem_call(
            functools.partial(stack_kernel, len(lanes + back)), "stack", lanes + back + order,
            [((len(lanes + back),) + own.shape, half)],
        )
        swapped.append(lax.ppermute(stacked, "orb", swap))
        if step >= steps - 2:
            slices += swapped
            swapped = []
    rows_sent, cut = [early_row], sent + 4
    for part in (slices[sent:cut], slices[cut:]):
        (row,) = vmem_call(row_kernel, "late_row", part, [((depth(part), nv), half)])
        rows_sent.append(lax.ppermute(row, "spin", across))
    fitted, amp_same, dens_same = vmem_call(
        fit_same_kernel, "fit_same", [occ_energy, virt_energy, factor, early] + slices[sent + 1 :],
        [((naux, count * nv), half), ((nv, count * nv), half), ((nv, nv), full)],
        [((nv, naux), half), ((nv, nv), full)],
    )
    rows = 2 * nv // orb_count
    share = (2, 2, rows, nv)
    amp_other, kept, sent = vmem_call(
        opposite_all_kernel, "opposite",
        [occ_energy, virt_energy, factor] + rows_sent + [fitted, dens_same],
        [((nv, count * nv), half)] + [(share, full)] * 2,
        [((nv, naux), half), ((nv, nv), full), ((nv, nv), full)],
        flops=pair * (naux + nv),
    )
    gamma_other = vmem_call(
        gamma_kernel, "gamma_other", [amp_other, fitted], [((nv // PIECES, naux), half)] * PIECES,
        flops=pair * naux,
    )
    (gamma_same,) = vmem_call(
        gamma_kernel, "gamma_same", [amp_same, fitted], [((nv, naux), full)], flops=2 * pair * naux
    )
    returned = [lax.ppermute(piece, "spin", across) for piece in gamma_other]
    arrived = lax.ppermute(sent, "orb", swap)
    one, two = vmem_call(near_kernel, "near", [kept, arrived] + list(gamma_other), [(share[1:], full)] * 2, [(share, full)])
    chip_moves = lambda first, second: [
        (d, 2 * (d // 2 ^ (second if d % 2 else first)) + d % 2) for d in range(orb_count)
    ]
    one = lax.ppermute(one, "orb", chip_moves(3, 1))
    two = lax.ppermute(two, "orb", chip_moves(0, 2))
    kept, sent = vmem_call(
        far_split_kernel, "far_split", [one, two], [(share[2:], full)] * 2, [(share[1:], full)]
    )
    arrived = lax.ppermute(sent, "orb", chip_moves(orb_count // 4, orb_count // 4))
    kept, sent = vmem_call(
        core_split_kernel, "core_split", [kept, arrived, gamma_same], [((rows // 2, nv), full)] * 2, [(share[2:], full)]
    )
    arrived = lax.ppermute(sent, "orb", swap)
    gamma, density = vmem_call(
        finish_kernel, "finish", [kept, arrived, gamma_same] + returned,
        [((nv, naux), full), ((1, rows // 2, nv), full)], pin=False,
    )
    return gamma[None, None], density


def fit_kernel(factor_ref, *refs):
    slices, out_ref = refs[:-1], refs[-1]
    for g in range(out_ref.shape[0]):
        raw = jnp.concatenate([piece[g] for piece in slices], axis=0)
        out_ref[g] = dot(factor_ref[...], raw, NN).astype(out_ref.dtype)


def fit(factor, slices, group):
    count, _, virt = slices[0].shape
    naux = factor.shape[0]
    return pl.pallas_call(
        fit_kernel,
        grid=(count // group,),
        in_specs=[pl.BlockSpec(factor.shape, lambda j: (0, 0))]
        + [pl.BlockSpec((group,) + s.shape[1:], lambda j: (j, 0, 0)) for s in slices],
        out_specs=pl.BlockSpec((group, naux, virt), lambda j: (j, 0, 0)),
        out_shape=jax.ShapeDtypeStruct((count, naux, virt), jnp.bfloat16),
        compiler_params=pltpu.CompilerParams(vmem_limit_bytes=VMEM_LIMIT),
        name="fit",
    )(factor, *slices)


def same_kernel(own_ref, pair_ref, own_block, blocks, v_col, v_row, gamma_ref, dens_ref, left):
    step = pl.program_id(0)

    @pl.when(step == 0)
    def _():
        left[...] = own_block[0].T
        gamma_ref[...] = jnp.zeros_like(gamma_ref)
        dens_ref[...] = jnp.zeros_like(dens_ref)

    group = blocks.shape[0]
    for g in range(group):
        right = blocks[g]
        coupling = dot(left[...], right, NN)
        coupling = coupling - coupling.T
        denominator = (pair_ref[step * group + g] - v_col[...]) - v_row[...]
        amplitude = (coupling / denominator).astype(jnp.bfloat16)
        gamma_ref[...] += dot(amplitude, right, NT)
        dens_ref[...] += 0.5 * dot(amplitude, amplitude, NT)


def same_spin(fitted, own_index, pair_energy, virt, group):
    count, naux, nv = fitted.shape
    whole = lambda shape: pl.BlockSpec(shape, lambda j, *_: (0,) * len(shape))
    return pl.pallas_call(
        same_kernel,
        grid_spec=pltpu.PrefetchScalarGridSpec(
            num_scalar_prefetch=2,
            grid=(count // group,),
            in_specs=[
                pl.BlockSpec((1, naux, nv), lambda j, own, pair: (own[0], 0, 0)),
                pl.BlockSpec((group, naux, nv), lambda j, own, pair: (j, 0, 0)),
                whole((nv, 1)),
                whole((1, nv)),
            ],
            out_specs=[whole((nv, naux)), whole((nv, nv))],
            scratch_shapes=[pltpu.VMEM((nv, naux), jnp.bfloat16)],
        ),
        out_shape=[
            jax.ShapeDtypeStruct((nv, naux), jnp.float32),
            jax.ShapeDtypeStruct((nv, nv), jnp.float32),
        ],
        compiler_params=pltpu.CompilerParams(vmem_limit_bytes=VMEM_LIMIT),
        name="same_spin",
    )(own_index, pair_energy, fitted, fitted, virt[:, None], virt[None, :])


def opposite_kernel(pair_ref, factor, raw, blocks, v_col, v_row, dens_in, gamma_ref, dens_ref, left):
    step = pl.program_id(0)

    @pl.when(step == 0)
    def _():
        left[...] = dot(factor[...], raw[...], NN).astype(left.dtype).T
        gamma_ref[...] = jnp.zeros_like(gamma_ref)
        dens_ref[...] = dens_in[...]

    group = blocks.shape[0]
    for g in range(group):
        right = blocks[g]
        coupling = dot(left[...], right, NN)
        denominator = (pair_ref[step * group + g] - v_col[...]) - v_row[...]
        amplitude = (coupling / denominator).astype(jnp.bfloat16)
        gamma_ref[...] += dot(amplitude, right, NT)
        dens_ref[...] += dot(amplitude, amplitude, TN)


def opposite_spin(fitted, factor, raw, pair_energy, virt_left, virt_right, dens, group):
    count, naux, nv = fitted.shape
    whole = lambda shape: pl.BlockSpec(shape, lambda j, *_: (0,) * len(shape))
    return pl.pallas_call(
        opposite_kernel,
        grid_spec=pltpu.PrefetchScalarGridSpec(
            num_scalar_prefetch=1,
            grid=(count // group,),
            in_specs=[
                whole(factor.shape),
                whole(raw.shape),
                pl.BlockSpec((group, naux, nv), lambda j, pair: (j, 0, 0)),
                whole((nv, 1)),
                whole((1, nv)),
                whole((nv, nv)),
            ],
            out_specs=[whole((nv, naux)), whole((nv, nv))],
            scratch_shapes=[pltpu.VMEM((nv, naux), jnp.bfloat16)],
        ),
        out_shape=[
            jax.ShapeDtypeStruct((nv, naux), jnp.float32),
            jax.ShapeDtypeStruct((nv, nv), jnp.float32),
        ],
        compiler_params=pltpu.CompilerParams(vmem_limit_bytes=VMEM_LIMIT),
        name="opposite_spin",
    )(pair_energy, factor, raw, fitted, virt_left[:, None], virt_right[None, :], dens)


def reduce_rows(total, orb_count, keep):
    index = lax.axis_index("orb")
    bits = orb_count.bit_length() - 1
    rows = total.reshape((2,) * (bits - 1) + total.shape[1:])
    for bit in range(1, bits + 1 - keep.bit_length()):
        axis = bits - 1 - bit
        mine = (index >> bit) & 1
        moves = [(d, d ^ (1 << bit)) for d in range(orb_count)]
        kept = lax.dynamic_index_in_dim(rows, mine, axis, keepdims=False)
        sent = lax.dynamic_index_in_dim(rows, 1 - mine, axis, keepdims=False)
        arrived = lax.ppermute(sent, "orb", moves)
        rows = kept + arrived
    return kept, arrived


def local_streamed(integrals, metric_factor, occ_energy, virt_energy, orb_count):
    spin_index = lax.axis_index("spin")
    orbit_index = lax.axis_index("orb")
    other_spin = 1 - spin_index
    pick = lambda array, n: lax.dynamic_index_in_dim(array, n, 0, keepdims=False)
    occ_same, occ_other = pick(occ_energy, spin_index), pick(occ_energy, other_spin)
    virt_same, virt_other = pick(virt_energy, spin_index), pick(virt_energy, other_spin)
    across = [(0, 1), (1, 0)]

    own = jnp.swapaxes(integrals[0], 1, 2)
    occupied, width, nv = own.shape
    naux = metric_factor.shape[0]
    sources = pick(jnp.asarray(slice_sources(orb_count)), orbit_index)
    factor = jnp.take(metric_factor.reshape(orb_count, width, naux), sources, axis=0)
    factor = factor.reshape(naux, naux).T

    slices = []
    for part in gather_slices(own, orb_count):
        slices += [part] if part.ndim == 3 else [part[n] for n in range(part.shape[0])]
    own_row = [pick(s, orbit_index) for s in slices]
    early = len(slices) - 6 if len(slices) > 8 else len(slices) // 2
    raw_row = jnp.concatenate(
        [
            lax.ppermute(jnp.concatenate(own_row[:early]), "spin", across),
            lax.ppermute(jnp.concatenate(own_row[early:]), "spin", across),
        ]
    )
    if width % 16:
        slices = [jnp.concatenate(slices, axis=1)]
    fitted = fit(factor, slices, 2)

    own_energy, other_energy = pick(occ_same, orbit_index), pick(occ_other, orbit_index)
    gamma_same, dens = same_spin(fitted, orbit_index[None], own_energy + occ_same, virt_same, 2)
    gamma_other, dens = opposite_spin(
        fitted, factor, raw_row, other_energy + occ_same, virt_other, virt_same, dens, 2
    )
    returned = lax.ppermute(gamma_other, "spin", across)
    gamma = gamma_same + returned
    split = dens.reshape(orb_count // 2, 2, nv // orb_count, nv) / occupied
    kept, sent = (lax.dynamic_index_in_dim(split, n, 1, False) for n in (orbit_index % 2, 1 - orbit_index % 2))
    swap = [(d, d ^ 1) for d in range(orb_count)]
    kept, arrived = reduce_rows(kept + lax.ppermute(sent, "orb", swap), orb_count, 1)
    density = kept + arrived
    return gamma[None, None], density[None]


def local(integrals, metric_factor, occ_energy, virt_energy, orb_count):
    _, count, nv, width = integrals.shape
    fits = orb_count // 2 == 4 * 2 and count * nv * metric_factor.shape[0] * 2 <= 4 * 1024 * 1024 and width % 16 == 0 and count % GROUP == 0
    chosen = local_in_vmem if fits else local_streamed
    return chosen(integrals, metric_factor, occ_energy, virt_energy, orb_count)


def solution(mesh):
    return jax.shard_map(
        functools.partial(local, orb_count=mesh.shape["orb"]),
        mesh=mesh,
        in_specs=(P("spin", None, None, "orb"), P(), P(), P()),
        out_specs=(P("spin", "orb", None, None), P("spin", "orb", None)),
        check_vma=False,
    )
```
